32 devices in a mesh: slab: 8 (over z, y), grp: 4 (over x, core).
Axes of the slice: x: 2, y: 2, z: 4, core: 2. Of those that a mesh axis runs over, the one named last changes fastest.
Arguments:
- tiles: bfloat16 [96, 27, 36864], P(('slab', 'grp')), may hold values from -0.0390625 to 0.0390625
- neighbours: int32 [96, 27], P('slab'), may hold values from 0 to 95, as said below
- t_cur: bfloat16 [96, 192, 512], P('slab', None, 'grp'), may hold values from -6 to 6
- t_prev: float32 [96, 192, 512], P('slab', None, 'grp'), may hold values from -6 to 6
- probes: float32 [96, 192, 512], P('slab', None, 'grp'), may hold values from -18 to 18
Outputs:
- t_next: float32 [96, 192, 512], P('slab', None, 'grp')
- moments: float32 [2, 512], P(None, 'grp')
The draws below stay inside these ranges and needn't reach their ends.
Inputs may be any that keep to these rules, and one draw needn't show every extreme that they name: Block b lies in slab b // 12; each of its neighbours lies in the same slab or in one of the two slabs beside it, the last slab being beside the first.
All inputs are finite; a program needn't handle non-finite values.
Results may differ from the reference program's by a relative error of at most 0.0003.
Values may be sent and summed in bfloat16 or wider, within the bound.
No kernel may reach another device: no remote copies, remote signals or barrier semaphores. Data moves between devices by JAX's collectives and lax.ppermute only.
A program may use at most 192 MiB of HBM per device.

```python
import math
import jax
import jax.numpy as jnp
from jax import lax

BS = 192
NEIGH = 27
BY = 3
BZ = 4
PROBES = 512
BPS = 12
NBLK = 96


def draw_neighbours(key, part):
    slabs = NBLK // BPS
    keys = jax.random.split(jax.random.fold_in(key, 11), slabs)
    perms = jax.vmap(lambda k: jax.random.permutation(k, BPS))(keys).astype(jnp.int32)
    inverse = jnp.argsort(perms, axis=1).astype(jnp.int32)
    block = jnp.arange(NBLK, dtype=jnp.int32)
    slab_of = block // BPS
    place = perms[slab_of, block % BPS]
    ycoord = place // BZ
    zcoord = place % BZ
    offs = jnp.arange(27, dtype=jnp.int32)
    shift_x = offs // 9 - 1
    shift_y = offs // 3 % 3 - 1
    shift_z = offs % 3 - 1
    near_slab = (slab_of[:, None] + shift_x[None, :]) % slabs
    near_place = (ycoord[:, None] + shift_y[None, :]) % BY * BZ + (zcoord[:, None] + shift_z[None, :]) % BZ
    near = near_slab * BPS + inverse[near_slab, near_place]
    okeys = jax.random.split(jax.random.fold_in(key, 12), NBLK)
    orders = jax.vmap(lambda k: jax.random.permutation(k, 27))(okeys).astype(jnp.int32)
    return jnp.take_along_axis(near, orders, axis=1).astype(jnp.int32)


def draw_probes(key, part):
    slabs = NBLK // BPS
    block = jnp.arange(NBLK, dtype=jnp.int32)
    ramp = 1.0 + 2.0 * (block // BPS).astype(jnp.float32) / (slabs - 1)
    ramp = ramp[:, None, None]
    base = jax.random.normal(jax.random.fold_in(key, 22), (NBLK, BS, PROBES), jnp.float32)
    values = jnp.clip(base, -6.0, 6.0) * ramp
    return values.astype(jnp.float32)


def block_levels(key, extent, pieces, smallest, top_value):
    level, own = 1.0, jax.random.fold_in(key, 6)
    for position, blocks in pieces:
        steps = jnp.exp(jax.random.uniform(jax.random.fold_in(own, position), (blocks,), jnp.float32, smallest / len(pieces), top_value / len(pieces)))
        level = level * jnp.repeat(steps, extent[position] // blocks).reshape([-1 if axis == position else 1 for axis in range(len(extent))])
    return level


def normal_values(key, dims, spread, limit, cuts=(), held_as=jnp.bfloat16):
    values = spread * jax.random.normal(key, dims, jnp.float32)
    if cuts:
        values = values * block_levels(key, dims, cuts, -0.22, 0.18)
    return jnp.clip(values, -limit, limit).astype(held_as)


def setup_inputs(seed: int = 0) -> dict:
    streams_of = jax.random.split(jax.random.key(seed), 6)
    return {
        "tiles": normal_values(streams_of[0], (NBLK, NEIGH, BS * BS), (4 * NEIGH * BS) ** -0.5, 0.0390625, ((0, 32),)),
        "neighbours": draw_neighbours(jax.random.fold_in(streams_of[5], 71), 0),
        "t_cur": normal_values(streams_of[2], (NBLK, BS, PROBES), 1.0, 6.0, ((0, 8), (2, 4))),
        "t_prev": normal_values(streams_of[3], (NBLK, BS, PROBES), 1.0, 6.0, ((0, 8), (2, 4)), jnp.float32),
        "probes": draw_probes(jax.random.fold_in(streams_of[5], 71), 0),
    }


def reference(tiles, neighbours, t_cur, t_prev, probes):
    current = t_cur.astype(jnp.float32)

    def one_block(pair):
        tile_row, nbr = pair
        square = tile_row.astype(jnp.float32).reshape((NEIGH, BS, BS))
        near = current[nbr.astype(jnp.int32)]
        return jnp.einsum('krc,kcp->rp', square, near)
    image = lax.map(one_block, (tiles, neighbours))
    t_next = 2.0 * image - t_prev
    factor = 1.0 / math.sqrt(NBLK * BS)
    first = lax.optimization_barrier(jnp.sum(probes * t_next, axis=(0, 1))) * factor
    second = lax.optimization_barrier(jnp.sum(current * t_next, axis=(0, 1))) * factor
    return (t_next, jnp.stack([first, second]))
```

```python
import functools
import math

import jax
import jax.numpy as jnp
from jax import lax
from jax.experimental import pallas as pl
from jax.experimental.pallas import tpu as pltpu
from jax.sharding import PartitionSpec as P

VMEM_LIMIT = 48 * 1024 * 1024


def image_kernel(ids, core, own_tiles, sib_tiles, *rest):
    nears, (own_img, oth_img, near) = rest[:6], rest[6:]
    step = pl.program_id(0)
    blocks, rows, cols = nears[0].shape
    pad = near.shape[1] - rows - 64
    neigh, half, wide = own_tiles.shape[1:]

    @pl.when(step == 0)
    def _():
        near[:, :64, :] = jnp.zeros((near.shape[0], 64, near.shape[2]), near.dtype)
        near[:, 64 + rows :, :] = jnp.zeros((near.shape[0], pad, near.shape[2]), near.dtype)
        for n, ref in enumerate(nears):
            at = (n % 3) * blocks
            side = (n // 3) * cols
            near[at : at + blocks, 64 : 64 + rows, side : side + cols] = ref[...]

    lane = lax.broadcasted_iota(jnp.int32, (half, 128), 1)

    def work(tiles):
        even = jnp.zeros((half, 2 * cols), jnp.float32)
        odd = jnp.zeros((half, 2 * cols), jnp.float32)
        for k in range(neigh):
            vec = near.at[ids[step * neigh + k]]
            tile = tiles[0, k]
            mid = tile[:, 128:256]
            none = jnp.zeros_like(mid)
            left = jnp.concatenate([tile[:, :128], jnp.where(lane < 64, mid, none)], axis=1)
            right = jnp.concatenate([jnp.where(lane < 64, none, mid), tile[:, 256:]], axis=1)
            even = even + jnp.dot(left, vec[64:, :], preferred_element_type=jnp.float32)
            odd = odd + jnp.dot(right, vec[: rows + 64, :], preferred_element_type=jnp.float32)
        for ref, side in ((own_img, 0), (oth_img, cols)):
            ref[0, pl.ds(0, half, 2), :] = even[:, side : side + cols]
            ref[0, pl.ds(1, half, 2), :] = odd[:, side : side + cols]

    @pl.when(step < own_tiles_steps(core))
    def _():
        work(own_tiles)

    @pl.when(step >= own_tiles_steps(core))
    def _():
        work(sib_tiles)


def own_tiles_steps(core):
    return core[1]


def images(ids, core, own_tiles, sib_tiles, nears):
    per, neigh, half, wide = own_tiles.shape
    blocks, rows, cols = nears[0].shape
    place = lambda b, ids, core: (jnp.where(b < per, core[0], 1 - core[0]) * per + b % per, 0, 0)
    tile = (1, neigh, half, wide)
    whole = pl.BlockSpec((blocks, rows, cols), lambda b, ids, core: (0, 0, 0))
    out = jax.ShapeDtypeStruct((2 * per, rows, cols), jnp.float32)
    return pl.pallas_call(
        image_kernel,
        grid_spec=pltpu.PrefetchScalarGridSpec(
            num_scalar_prefetch=2,
            grid=(2 * per,),
            in_specs=[
                pl.BlockSpec(tile, lambda b, ids, core: (jnp.minimum(b, per - 1), 0, 0, 0)),
                pl.BlockSpec(tile, lambda b, ids, core: (jnp.maximum(b - per, 0), 0, 0, 0)),
            ]
            + [whole] * 6,
            out_specs=[pl.BlockSpec((1, rows, cols), place)] * 2,
            scratch_shapes=[pltpu.VMEM((3 * blocks, rows + 128, 2 * cols), jnp.bfloat16)],
        ),
        out_shape=[out, out],
        compiler_params=pltpu.CompilerParams(vmem_limit_bytes=VMEM_LIMIT),
        name="images",
    )(ids, core, own_tiles, sib_tiles, *nears)


def next_kernel(side, own_img, oth_img, prev, probes, cur, out, sums):
    step = pl.program_id(0)

    def work(img):
        value = 2.0 * img[...] - prev[...]
        out[...] = value
        first = probes[...] * value
        second = cur[...].astype(jnp.float32) * value
        for n, term in enumerate((first, second)):
            part = jnp.sum(term.reshape(-1, 8, term.shape[-1]), axis=0)
            at = pl.ds(8 * n, 8)
            sums[at, :] = jnp.where(step == 0, part, sums[at, :] + part)

    @pl.when(step < pl.num_programs(0) // 2)
    def _():
        work(own_img)

    @pl.when(step >= pl.num_programs(0) // 2)
    def _():
        work(oth_img)


def next_vectors(side, own_img, oth_img, prev, probes, cur):
    half, rows, cols = own_img.shape
    parts = 2
    size = half // parts
    block = (size, rows, cols)
    spot = lambda i, side: (jnp.where(i < parts, side[0], 1 - side[0]) * parts + i % parts, 0, 0)
    return pl.pallas_call(
        next_kernel,
        grid_spec=pltpu.PrefetchScalarGridSpec(
            num_scalar_prefetch=1,
            grid=(2 * parts,),
            in_specs=[
                pl.BlockSpec(block, lambda i, side: (jnp.minimum(i, parts - 1), 0, 0)),
                pl.BlockSpec(block, lambda i, side: (jnp.maximum(i - parts, 0), 0, 0)),
            ]
            + [pl.BlockSpec(block, spot)] * 3,
            out_specs=[pl.BlockSpec(block, spot), pl.BlockSpec((16, cols), lambda i, side: (0, 0))],
        ),
        out_shape=[
            jax.ShapeDtypeStruct(prev.shape, jnp.float32),
            jax.ShapeDtypeStruct((16, cols), jnp.float32),
        ],
        compiler_params=pltpu.CompilerParams(vmem_limit_bytes=VMEM_LIMIT),
        name="next_vectors",
    )(side, own_img, oth_img, prev, probes, cur)


def sum_over(value, axis):
    size = lax.axis_size(axis)
    if size & (size - 1):
        return lax.psum(value, axis)
    hop = 1
    while hop < size:
        value = value + lax.ppermute(value, axis, [(i, i ^ hop) for i in range(size)])
        hop *= 2
    return value


def shards(tiles, neighbours, t_cur, t_prev, probes):
    blocks, rows, cols = t_cur.shape
    per, neigh = tiles.shape[:2]
    slabs, lanes = lax.axis_size("slab"), lax.axis_size("grp")
    slab, lane = lax.axis_index("slab"), lax.axis_index("grp")
    side, core = lane // 2, lane % 2
    across = functools.partial(lax.ppermute, axis_name="grp", perm=[(i, i ^ 2) for i in range(lanes)])
    sibling = functools.partial(lax.ppermute, axis_name="grp", perm=[(i, i ^ 1) for i in range(lanes)])
    pair = functools.partial(lax.ppermute, axis_name="slab", perm=[(i, i ^ 1) for i in range(slabs)])
    along = functools.partial(
        lax.ppermute,
        axis_name="slab",
        perm=[(i, (i + 2 if i % 2 == 0 else i - 2) % slabs) for i in range(slabs)],
    )

    oth = across(t_cur)
    near_own = pair(t_cur)
    squares = tiles.reshape(per, neigh, rows // 2, 2 * rows)
    sib_squares = sibling(squares)
    near_oth = pair(oth)
    far_own = along(near_own)
    far_oth = along(near_oth)

    owner = neighbours // blocks
    kind = jnp.where(owner == slab, 0, jnp.where(owner == slab ^ 1, 1, 2))
    local = (kind * blocks + neighbours % blocks).astype(jnp.int32)
    mine = lax.dynamic_slice_in_dim(local, lane * per, per, 0)
    theirs = lax.dynamic_slice_in_dim(local, (lane ^ 1) * per, per, 0)
    ids = jnp.concatenate([mine, theirs]).reshape(-1)

    own_img, oth_img = images(
        ids,
        jnp.stack([core, jnp.int32(per)]).astype(jnp.int32),
        squares,
        sib_squares,
        (t_cur, near_own, far_own, oth, near_oth, far_oth),
    )
    back = across(oth_img)
    t_next, sums = next_vectors(side.astype(jnp.int32)[None], own_img, back, t_prev, probes, t_cur)
    sums = jnp.sum(sums.reshape(2, 8, cols), axis=1)
    factor = 1.0 / math.sqrt(slabs * blocks * rows)
    moments = sum_over(sums, "slab") * factor
    return (t_next, moments)


def solution(mesh):
    placed = (
        P(("slab", "grp"), None, None),
        P("slab", None),
        P("slab", None, "grp"),
        P("slab", None, "grp"),
        P("slab", None, "grp"),
    )
    return jax.shard_map(
        shards,
        mesh=mesh,
        in_specs=placed,
        out_specs=(P("slab", None, "grp"), P(None, "grp")),
        check_vma=False,
    )
```

```python
import functools
import math

import jax
import jax.numpy as jnp
from jax import lax
from jax.experimental import pallas as pl
from jax.experimental.pallas import tpu as pltpu
from jax.sharding import PartitionSpec as P

GRANT = 20 * 1024 * 1024
BLOCKS = 6
PAD = 64
LIGHT = pl.CostEstimate(flops=1, bytes_accessed=1, transcendentals=0)
HEAVY = pl.CostEstimate(flops=1, bytes_accessed=18_000_000, transcendentals=0)
VMEM = pl.BlockSpec(memory_space=pltpu.VMEM)
SMEM = pl.BlockSpec(memory_space=pltpu.SMEM)
HBM = pl.BlockSpec(memory_space=pltpu.HBM)
ANY = pl.BlockSpec(memory_space=pl.ANY)
DMA = pltpu.SemaphoreType.DMA


def in_vmem(arrays):
    return [pltpu.with_memory_space_constraint(a, pltpu.VMEM) for a in arrays]


def in_smem(table):
    return pltpu.with_memory_space_constraint(table, pltpu.SMEM)


def in_hbm(arrays):
    return [pltpu.with_memory_space_constraint(a, pltpu.HBM) for a in arrays]


def params():
    return pltpu.CompilerParams(vmem_limit_bytes=GRANT)


def copy(src, dst, sem):
    made = pltpu.make_async_copy(src, dst, sem)
    made.start()
    return made


def meets_kernel(neighbours, out, table, sem):
    blocks, neigh = neighbours.shape
    slab, lane = lax.axis_index("slab"), lax.axis_index("grp")
    per = BLOCKS // 2
    table[...] = jnp.zeros_like(table)
    for side, first in enumerate((lane * per, (lane ^ 1) * per)):
        for n in range(per):
            table[pl.ds(side * per + n, 1), :neigh] = neighbours[pl.ds(first + n, 1), :]
    mine = table[...]
    owner = mine // blocks
    kind = jnp.where(owner == slab, 0, jnp.where(owner == (slab ^ 1), 1, 2))
    table[...] = kind * blocks + mine - owner * blocks
    copy(table, out, sem).wait()


def meets(neighbours):
    return pl.pallas_call(
        meets_kernel,
        in_specs=[VMEM],
        out_specs=SMEM,
        out_shape=pltpu.SMEM((8, 128), jnp.int32),
        scratch_shapes=[pltpu.VMEM((8, 128), jnp.int32), DMA],
        compiler_params=params(),
        cost_estimate=LIGHT,
        name="meets",
    )(neighbours)


def square_part(src, held, low):
    neigh, wide = src.shape[0], held.shape[2]
    piece = [src[:, pl.ds(pl.multiple_of(j * wide, wide), wide)] for j in range(16)]
    held[:, pl.ds(low, 16), :] = jnp.transpose(jnp.stack(piece, axis=0), (1, 0, 2))


def square_kernel(parts, tiles, held, raw, sems):
    count, _, half, wide = held.shape
    each = parts // count
    size = half // each
    loads = []
    for n in range(parts):
        src = tiles.at[n // each, :, pl.ds((n % each) * size * wide, size * wide)]
        loads.append(copy(src, raw.at[n], sems.at[n]))
    for n in range(parts):
        loads[n].wait()

        @pl.loop(0, size // 16)
        def _(step):
            low = pl.multiple_of((n % each) * size + step * 16, 16)
            src = raw.at[n, :, pl.ds(pl.multiple_of(step * 16 * wide, 128), 16 * wide)]
            square_part(src, held.at[n // each], low)


def held_kernel(tiles, held):
    count, _, half, wide = held.shape

    @pl.loop(0, count * (half // 16))
    def _(step):
        b, part = step // (half // 16), step % (half // 16)
        src = tiles.at[b, :, pl.ds(pl.multiple_of(part * 16 * wide, 128), 16 * wide)]
        square_part(src, held.at[b], pl.multiple_of(part * 16, 16))


def squares(tiles, rows, resident):
    count, neigh = tiles.shape[:2]
    half, wide = rows // 2, 2 * rows
    parts = 3 * count
    raw = [pltpu.VMEM((parts, neigh, rows * rows // 3), tiles.dtype), DMA((parts,))]
    return pl.pallas_call(
        held_kernel if resident else functools.partial(square_kernel, parts),
        in_specs=[VMEM if resident else HBM],
        out_specs=VMEM,
        out_shape=pltpu.VMEM((count, neigh, half, wide), tiles.dtype),
        scratch_shapes=[] if resident else raw,
        compiler_params=params(),
        cost_estimate=HEAVY,
        name="squares",
    )(*(in_vmem([tiles]) if resident else in_hbm([tiles])))


def start_near(chunks, near, sems):
    copies, at = [], 0
    for n, chunk in enumerate(chunks):
        copies.append(copy(chunk, near.at[pl.ds(at, chunk.shape[0])], sems.at[n]))
        at += chunk.shape[0]
    return copies


def multiply(tiles, table, row, near):
    count, half, wide = tiles.shape
    rows = wide // 2
    lane = lax.broadcasted_iota(jnp.int32, (half, 128), 1)
    even = odd = None
    for k in range(count):
        vec = near[table[row, k]]
        tile = tiles[k]
        mid = tile[:, 128:256]
        none = jnp.zeros_like(mid)
        left = jnp.concatenate([tile[:, :128], jnp.where(lane < PAD, mid, none)], axis=1)
        right = jnp.concatenate([jnp.where(lane < PAD, none, mid), tile[:, 256:]], axis=1)
        one = jnp.concatenate([vec, vec[:PAD]], axis=0)
        two = jnp.concatenate([vec[rows - PAD :], vec], axis=0)
        one = jnp.dot(left, one, preferred_element_type=jnp.float32)
        two = jnp.dot(right, two, preferred_element_type=jnp.float32)
        even = one if even is None else even + one
        odd = two if odd is None else odd + two
    return even, odd


def each_block(held, body):
    first = 0
    for square in held:
        start = first

        @pl.loop(0, square.shape[0])
        def _(n):
            body(start + n, square.at[n])

        first += square.shape[0]


def place(b):
    per = BLOCKS // 2
    core = lax.axis_index("grp") % 2
    return jnp.where(b < per, core * per + b, (1 - core) * per + b - per)


def near_scratch(chunks):
    return pltpu.VMEM((sum(c.shape[0] for c in chunks),) + chunks[0].shape[1:], chunks[0].dtype)


def other_kernel(n_chunks, table, first, second, *refs):
    chunks = refs[:n_chunks]
    out, near, image, near_sems, out_sems = refs[-5:]
    half = first.shape[2]
    for load in start_near(chunks, near, near_sems):
        load.wait()

    def body(b, tiles):
        even, odd = multiply(tiles, table, b, near)
        image[b, pl.ds(0, half, 2), :] = even
        image[b, pl.ds(1, half, 2), :] = odd
        copy(image.at[b], out.at[place(b)], out_sems.at[b])

    each_block((first, second), body)
    for b in range(BLOCKS):
        pltpu.make_async_copy(image.at[b], out.at[place(b)], out_sems.at[b]).wait()


def other_images(table, held, chunks, after):
    rows, cols = chunks[0].shape[1:]
    return pl.pallas_call(
        functools.partial(other_kernel, len(chunks)),
        in_specs=[SMEM] + [VMEM] * 2 + [ANY] * (len(chunks) + len(after)),
        out_specs=HBM,
        out_shape=pltpu.HBM((BLOCKS, rows, cols), jnp.float32),
        scratch_shapes=[
            near_scratch(chunks),
            pltpu.VMEM((BLOCKS, rows, cols), jnp.float32),
            DMA((len(chunks),)),
            DMA((BLOCKS,)),
        ],
        compiler_params=params(),
        cost_estimate=HEAVY,
        name="other_images",
    )(in_smem(table), *in_vmem(held), *chunks, *after)


def add_sums(factor, value, probes, cur, sums):
    for n, term in enumerate((probes * value, cur.astype(jnp.float32) * value)):
        part = jnp.sum(term.reshape(-1, 8, term.shape[-1]), axis=0) * factor
        sums[pl.ds(8 * n, 8), :] += part


def own_kernel(n_chunks, factor, table, first_held, second_held, *refs):
    chunks, rows_in = refs[:n_chunks], refs[n_chunks : n_chunks + 3]
    out, sums, near, held, image, prev, probes, cur, near_sems, held_sems, row_sems, out_sems = refs[-12:]
    half = first_held.shape[2]
    loads = start_near(chunks, near, near_sems)
    slots = held.shape[0]

    def load(n, square):
        return pltpu.make_async_copy(square, held.at[n % slots], held_sems.at[n % slots])

    def load_next(n):
        count = first_held.shape[0]
        pl.when(n < count)(lambda: load(n, first_held.at[jnp.minimum(n, count - 1)]).start())
        more = (n >= count) & (n < BLOCKS)
        pl.when(more)(lambda: load(n, second_held.at[jnp.clip(n - count, 0, BLOCKS - count - 1)]).start())

    for n in range(slots - 1):
        load_next(n)
    first = (lax.axis_index("grp") // 2) * BLOCKS
    for n, (src, dst) in enumerate(zip(rows_in, (prev, probes, cur))):
        loads.append(copy(src.at[pl.ds(first, BLOCKS)], dst, row_sems.at[n]))
    sums[...] = jnp.zeros_like(sums)
    for made in loads:
        made.wait()

    @pl.loop(0, BLOCKS)
    def _(b):
        load_next(b + slots - 1)
        load(b, first_held.at[0]).wait()
        at = place(b)
        even, odd = multiply(held.at[b % slots], table, b, near)
        image[b, pl.ds(0, half, 2), :] = even
        image[b, pl.ds(1, half, 2), :] = odd
        value = 2.0 * image[b] - prev[at]
        image[b] = value
        copy(image.at[b], out.at[first + at], out_sems.at[b])
        add_sums(factor, value, probes[at], cur[at], sums)

    for b in range(BLOCKS):
        pltpu.make_async_copy(image.at[b], out.at[first + place(b)], out_sems.at[b]).wait()


def own_rows(table, held, chunks, factor, prev, probes, cur, after):
    rows, cols = cur.shape[1:]
    part = (BLOCKS, rows, cols)
    return pl.pallas_call(
        functools.partial(own_kernel, len(chunks), factor),
        in_specs=[SMEM] + [HBM] * 2 + [ANY] * (len(chunks) + 3 + len(after)),
        out_specs=[HBM, VMEM],
        out_shape=[
            jax.ShapeDtypeStruct(prev.shape, jnp.float32),
            jax.ShapeDtypeStruct((16, cols), jnp.float32),
        ],
        scratch_shapes=[
            near_scratch(chunks),
            pltpu.VMEM((3,) + held[0].shape[1:], held[0].dtype),
            pltpu.VMEM(part, jnp.float32),
            pltpu.VMEM(part, jnp.float32),
            pltpu.VMEM(part, jnp.float32),
            pltpu.VMEM(part, cur.dtype),
            DMA((len(chunks),)),
            DMA((3,)),
            DMA((3,)),
            DMA((BLOCKS,)),
        ],
        compiler_params=params(),
        cost_estimate=HEAVY,
        name="own_rows",
    )(in_smem(table), *in_hbm(held), *chunks, prev, probes, cur, *after)


def final_kernel(factor, side, image, prev, probes, cur, _, sums_in, out, sums, acc):
    step = pl.program_id(0)

    @pl.when(step == 0)
    def _():
        acc[...] = sums_in[...]

    value = 2.0 * image[...] - prev[...]
    out[...] = value
    add_sums(factor, value, probes[...], cur[...], acc)

    @pl.when(step == pl.num_programs(0) - 1)
    def _():
        for n in range(2):
            sums[pl.ds(n, 1), :] = jnp.sum(acc[pl.ds(8 * n, 8), :], axis=0, keepdims=True)


def other_rows(side, factor, image, prev, probes, cur, t_next, sums):
    half, rows, cols = image.shape
    steps = 3
    block = (half // steps, rows, cols)
    spot = pl.BlockSpec(block, lambda i, side: ((1 - side[0]) * steps + i, 0, 0))
    return pl.pallas_call(
        functools.partial(final_kernel, factor),
        grid_spec=pltpu.PrefetchScalarGridSpec(
            num_scalar_prefetch=1,
            grid=(steps,),
            in_specs=[pl.BlockSpec(block, lambda i, side: (i, 0, 0))]
            + [spot] * 3
            + [pl.BlockSpec(memory_space=pl.ANY), pl.BlockSpec((16, cols), lambda i, side: (0, 0))],
            out_specs=[spot, pl.BlockSpec((2, cols), lambda i, side: (0, 0))],
            scratch_shapes=[pltpu.VMEM((16, cols), jnp.float32)],
        ),
        out_shape=[
            jax.ShapeDtypeStruct(prev.shape, jnp.float32),
            jax.ShapeDtypeStruct((2, cols), jnp.float32),
        ],
        input_output_aliases={5: 0},
        compiler_params=params(),
        cost_estimate=LIGHT,
        name="other_rows",
    )(side, image, prev, probes, cur, t_next, sums)


def gate(value, *after):
    return pl.pallas_call(
        lambda *refs: None,
        in_specs=[ANY] * (1 + len(after)),
        out_specs=ANY,
        out_shape=jax.ShapeDtypeStruct(value.shape, value.dtype),
        input_output_aliases={0: 0},
        compiler_params=params(),
        cost_estimate=LIGHT,
        name="gate",
    )(value, *after)


def sum_over(value, axis):
    size = lax.axis_size(axis)
    if size & (size - 1):
        return lax.psum(value, axis)
    hop = 1
    while hop < size:
        value = value + lax.ppermute(value, axis, [(i, i ^ hop) for i in range(size)])
        hop *= 2
    return value


def shards(tiles, neighbours, t_cur, t_prev, probes):
    blocks, rows, cols = t_cur.shape
    per = tiles.shape[0]
    slabs, lanes = lax.axis_size("slab"), lax.axis_size("grp")
    side = (lax.axis_index("grp") // 2).astype(jnp.int32)[None]
    factor = 1.0 / math.sqrt(slabs * blocks * rows)
    across = functools.partial(lax.ppermute, axis_name="grp", perm=[(i, i ^ 2) for i in range(lanes)])
    sibling = functools.partial(lax.ppermute, axis_name="grp", perm=[(i, i ^ 1) for i in range(lanes)])
    pair = functools.partial(lax.ppermute, axis_name="slab", perm=[(i, i ^ 1) for i in range(slabs)])
    along = functools.partial(
        lax.ppermute,
        axis_name="slab",
        perm=[(i, (i + 2 if i % 2 == 0 else i - 2) % slabs) for i in range(slabs)],
    )

    tiles, t_prev, probes, fixed = in_hbm([tiles, t_prev, probes, t_cur])
    half = blocks // 2
    low, high = t_cur[:half], t_cur[half:]

    sib_tiles = sibling(tiles)
    oth = [across(low), across(high)]
    near_high = pair(high)
    table = meets(neighbours)
    held = [squares(tiles, rows, False)]
    near_oth = [pair(gate(oth[0], *held)), pair(oth[1])]
    far_high = along(near_high)
    far_oth = [along(near_oth[0]), across(far_high)]
    held.append(squares(sib_tiles, rows, True))
    near_low = pair(gate(low, held[1]))
    far_low = along(near_low)

    images = other_images(table, held, [*oth, *near_oth, *far_oth], ())
    back = across(images)
    own = [fixed, near_low, near_high, far_low, far_high]
    t_next, sums = own_rows(table, held, own, factor, t_prev, probes, fixed, in_hbm([images]))
    t_next, sums = other_rows(side, factor, back, t_prev, probes, fixed, t_next, sums)
    return (t_next, sum_over(sums, "slab"))


def solution(mesh):
    placed = (
        P(("slab", "grp"), None, None),
        P("slab", None),
        P("slab", None, "grp"),
        P("slab", None, "grp"),
        P("slab", None, "grp"),
    )
    return jax.shard_map(
        shards,
        mesh=mesh,
        in_specs=placed,
        out_specs=(P("slab", None, "grp"), P(None, "grp")),
        check_vma=False,
    )
```

```python
import functools
import math

import jax
import jax.numpy as jnp
from jax import lax
from jax.experimental import pallas as pl
from jax.experimental.pallas import tpu as pltpu
from jax.sharding import PartitionSpec as P

GRANT = 20 * 1024 * 1024
BLOCKS = 6
PAD = 64
LEVELS = 32760.0
LIGHT = pl.CostEstimate(flops=1, bytes_accessed=1, transcendentals=0)
LONG = pl.CostEstimate(flops=1, bytes_accessed=1_000_000_000, transcendentals=0)
HEAVY = pl.CostEstimate(flops=1, bytes_accessed=18_000_000, transcendentals=0)
VMEM = pl.BlockSpec(memory_space=pltpu.VMEM)
SMEM = pl.BlockSpec(memory_space=pltpu.SMEM)
HBM = pl.BlockSpec(memory_space=pltpu.HBM)
ANY = pl.BlockSpec(memory_space=pl.ANY)
DMA = pltpu.SemaphoreType.DMA


def in_vmem(arrays):
    return [pltpu.with_memory_space_constraint(a, pltpu.VMEM) for a in arrays]


def in_smem(table):
    return pltpu.with_memory_space_constraint(table, pltpu.SMEM)


def in_hbm(arrays):
    return [pltpu.with_memory_space_constraint(a, pltpu.HBM) for a in arrays]


def params():
    return pltpu.CompilerParams(vmem_limit_bytes=GRANT)


def copy(src, dst, sem):
    made = pltpu.make_async_copy(src, dst, sem)
    made.start()
    return made


def meets_kernel(neighbours, out, table, sem):
    blocks, neigh = neighbours.shape
    slab, lane = lax.axis_index("slab"), lax.axis_index("grp")
    per = BLOCKS // 2
    table[...] = jnp.zeros_like(table)
    for side, first in enumerate((lane * per, (lane ^ 1) * per)):
        for n in range(per):
            table[pl.ds(side * per + n, 1), :neigh] = neighbours[pl.ds(first + n, 1), :]
    mine = table[...]
    owner = mine // blocks
    kind = jnp.where(owner == slab, 0, jnp.where(owner == (slab ^ 1), 1, 2))
    table[...] = kind * blocks + mine - owner * blocks
    copy(table, out, sem).wait()


def meets(neighbours):
    return pl.pallas_call(
        meets_kernel,
        in_specs=[VMEM],
        out_specs=SMEM,
        out_shape=pltpu.SMEM((8, 128), jnp.int32),
        scratch_shapes=[pltpu.VMEM((8, 128), jnp.int32), DMA],
        compiler_params=params(),
        cost_estimate=LIGHT,
        name="meets",
    )(neighbours)


def square_part(src, held, low):
    neigh, wide = src.shape[0], held.shape[2]
    piece = [src[:, pl.ds(pl.multiple_of(j * wide, wide), wide)] for j in range(16)]
    held[:, pl.ds(low, 16), :] = jnp.transpose(jnp.stack(piece, axis=0), (1, 0, 2))


def square_kernel(parts, tiles, held, raw, sems):
    count, _, half, wide = held.shape
    each = parts // count
    size = half // each
    loads = []
    for n in range(parts):
        src = tiles.at[n // each, :, pl.ds((n % each) * size * wide, size * wide)]
        loads.append(copy(src, raw.at[n], sems.at[n]))
    for n in range(parts):
        loads[n].wait()

        @pl.loop(0, size // 16)
        def _(step):
            low = pl.multiple_of((n % each) * size + step * 16, 16)
            src = raw.at[n, :, pl.ds(pl.multiple_of(step * 16 * wide, 128), 16 * wide)]
            square_part(src, held.at[n // each], low)


def held_kernel(tiles, held):
    count, _, half, wide = held.shape

    @pl.loop(0, count * (half // 16))
    def _(step):
        b, part = step // (half // 16), step % (half // 16)
        src = tiles.at[b, :, pl.ds(pl.multiple_of(part * 16 * wide, 128), 16 * wide)]
        square_part(src, held.at[b], pl.multiple_of(part * 16, 16))


def squares(tiles, rows, resident):
    count, neigh = tiles.shape[:2]
    half, wide = rows // 2, 2 * rows
    parts = 3 * count
    raw = [pltpu.VMEM((parts, neigh, rows * rows // 3), tiles.dtype), DMA((parts,))]
    return pl.pallas_call(
        held_kernel if resident else functools.partial(square_kernel, parts),
        in_specs=[VMEM if resident else HBM],
        out_specs=VMEM,
        out_shape=pltpu.VMEM((count, neigh, half, wide), tiles.dtype),
        scratch_shapes=[] if resident else raw,
        compiler_params=params(),
        cost_estimate=HEAVY,
        name="squares",
    )(*(in_vmem([tiles]) if resident else in_hbm([tiles])))


def start_near(chunks, near, sems):
    copies, at = [], 0
    for n, chunk in enumerate(chunks):
        copies.append(copy(chunk, near.at[pl.ds(at, chunk.shape[0])], sems.at[n]))
        at += chunk.shape[0]
    return copies


def multiply(tiles, table, row, near):
    count, half, wide = tiles.shape
    rows = wide // 2
    lane = lax.broadcasted_iota(jnp.int32, (half, 128), 1)
    even = odd = None
    for k in range(count):
        vec = near[table[row, k]]
        tile = tiles[k]
        mid = tile[:, 128:256]
        none = jnp.zeros_like(mid)
        left = jnp.concatenate([tile[:, :128], jnp.where(lane < PAD, mid, none)], axis=1)
        right = jnp.concatenate([jnp.where(lane < PAD, none, mid), tile[:, 256:]], axis=1)
        one = jnp.concatenate([vec, vec[:PAD]], axis=0)
        two = jnp.concatenate([vec[rows - PAD :], vec], axis=0)
        one = jnp.dot(left, one, preferred_element_type=jnp.float32)
        two = jnp.dot(right, two, preferred_element_type=jnp.float32)
        even = one if even is None else even + one
        odd = two if odd is None else odd + two
    return even, odd


def each_block(held, body):
    first = 0
    for square in held:
        start = first

        @pl.loop(0, square.shape[0])
        def _(n):
            body(start + n, square.at[n])

        first += square.shape[0]


def place(b):
    per = BLOCKS // 2
    core = lax.axis_index("grp") % 2
    return jnp.where(b < per, core * per + b, (1 - core) * per + b - per)


def near_scratch(chunks):
    return pltpu.VMEM((sum(c.shape[0] for c in chunks),) + chunks[0].shape[1:], chunks[0].dtype)


def largest(power, size):
    return size * jnp.exp2(power - 14.0)


def other_kernel(n_chunks, table, first, second, *refs):
    chunks = refs[:n_chunks]
    out, near, image, coded, scales, near_sems, out_sems = refs[-7:]
    half, rows = first.shape[2], image.shape[0]
    scales[...] = jnp.zeros_like(scales)
    for load in start_near(chunks, near, near_sems):
        load.wait()

    def send(b):
        rows_out = out.at[pl.ds(pl.multiple_of(place(b) * rows, rows), rows)]
        return pltpu.make_async_copy(coded.at[b], rows_out, out_sems.at[b])

    def body(b, tiles):
        even, odd = multiply(tiles, table, b, near)
        image[pl.ds(0, half, 2), :] = even
        image[pl.ds(1, half, 2), :] = odd
        value = image[...]
        top = jnp.maximum(jnp.max(jnp.abs(value), axis=0, keepdims=True), 1e-30)
        power = jnp.ceil(jnp.log2(top))
        size = jnp.ceil(top * jnp.exp2(14.0 - power))
        scales[pl.ds(place(b), 1), :] = power
        scales[pl.ds(8 + place(b), 1), :] = size
        value = jnp.round(value * (LEVELS / largest(power, size)))
        coded[b] = value.astype(jnp.int32).astype(jnp.int16)
        send(b).start()

    each_block((first, second), body)
    coded[BLOCKS, :16, :] = scales[...].astype(jnp.int32).astype(jnp.int16)
    last = copy(coded.at[BLOCKS, pl.ds(0, 16)], out.at[pl.ds(BLOCKS * rows, 16)], out_sems.at[BLOCKS])
    for b in range(BLOCKS):
        send(b).wait()
    last.wait()


def other_images(table, held, chunks, after):
    rows, cols = chunks[0].shape[1:]
    return pl.pallas_call(
        functools.partial(other_kernel, len(chunks)),
        in_specs=[SMEM] + [VMEM] * 2 + [ANY] * (len(chunks) + len(after)),
        out_specs=HBM,
        out_shape=pltpu.HBM((BLOCKS * rows + 16, cols), jnp.int16),
        scratch_shapes=[
            near_scratch(chunks),
            pltpu.VMEM((rows, cols), jnp.float32),
            pltpu.VMEM((BLOCKS + 1, rows, cols), jnp.int16),
            pltpu.VMEM((16, cols), jnp.float32),
            DMA((len(chunks),)),
            DMA((BLOCKS + 1,)),
        ],
        compiler_params=params(),
        cost_estimate=LONG,
        name="other_images",
    )(in_smem(table), *in_vmem(held), *chunks, *after)


def add_sums(factor, value, probes, cur, sums):
    for n, term in enumerate((probes * value, cur.astype(jnp.float32) * value)):
        part = jnp.sum(term.reshape(-1, 8, term.shape[-1]), axis=0) * factor
        sums[pl.ds(8 * n, 8), :] += part


def own_kernel(n_chunks, factor, table, first_held, second_held, *refs):
    chunks, rows_in = refs[:n_chunks], refs[n_chunks : n_chunks + 3]
    out, sums, *later = refs[n_chunks + 4 : n_chunks + 9]
    near, held, image, prev, probes, cur, near_sems, held_sems, row_sems, later_sems, out_sems = refs[-11:]
    half = first_held.shape[2]
    loads = start_near(chunks, near, near_sems)
    slots = held.shape[0]

    def load(n, square):
        return pltpu.make_async_copy(square, held.at[n % slots], held_sems.at[n % slots])

    def load_next(n):
        count = first_held.shape[0]
        pl.when(n < count)(lambda: load(n, first_held.at[jnp.minimum(n, count - 1)]).start())
        more = (n >= count) & (n < BLOCKS)
        pl.when(more)(lambda: load(n, second_held.at[jnp.clip(n - count, 0, BLOCKS - count - 1)]).start())

    for n in range(slots - 1):
        load_next(n)
    first = (lax.axis_index("grp") // 2) * BLOCKS
    mine = []
    for n, (src, dst) in enumerate(zip(rows_in, (prev, probes, cur))):
        mine.append(copy(src.at[pl.ds(first, BLOCKS)], dst, row_sems.at[n]))
    sums[...] = jnp.zeros_like(sums)
    for made in loads:
        made.wait()

    @pl.loop(0, BLOCKS)
    def _(b):
        load_next(b + slots - 1)
        load(b, first_held.at[0]).wait()
        at = place(b)
        even, odd = multiply(held.at[b % slots], table, b, near)

        @pl.when(b == 0)
        def _():
            for made in mine:
                made.wait()
            for n, (src, dst) in enumerate(zip(rows_in, later)):
                copy(src.at[pl.ds(BLOCKS - first, BLOCKS)], dst, later_sems.at[n])

        image[b, pl.ds(0, half, 2), :] = even
        image[b, pl.ds(1, half, 2), :] = odd
        value = 2.0 * image[b] - prev[at]
        image[b] = value
        copy(image.at[b], out.at[first + at], out_sems.at[b])
        add_sums(factor, value, probes[at], cur[at], sums)

    for n, (src, dst) in enumerate(zip(rows_in, later)):
        pltpu.make_async_copy(src.at[pl.ds(BLOCKS - first, BLOCKS)], dst, later_sems.at[n]).wait()
    for b in range(BLOCKS):
        pltpu.make_async_copy(image.at[b], out.at[first + place(b)], out_sems.at[b]).wait()


def own_rows(table, held, chunks, factor, prev, probes, cur, after):
    rows, cols = cur.shape[1:]
    part = (BLOCKS, rows, cols)
    return pl.pallas_call(
        functools.partial(own_kernel, len(chunks), factor),
        in_specs=[SMEM] + [HBM] * 2 + [ANY] * (len(chunks) + 3 + len(after)),
        out_specs=[HBM] + [VMEM] * 4,
        out_shape=[
            pltpu.HBM(prev.shape, jnp.float32),
            pltpu.VMEM((16, cols), jnp.float32),
            pltpu.VMEM(part, jnp.float32),
            pltpu.VMEM(part, jnp.float32),
            pltpu.VMEM(part, cur.dtype),
        ],
        scratch_shapes=[
            near_scratch(chunks),
            pltpu.VMEM((3,) + held[0].shape[1:], held[0].dtype),
            pltpu.VMEM(part, jnp.float32),
            pltpu.VMEM(part, jnp.float32),
            pltpu.VMEM(part, jnp.float32),
            pltpu.VMEM(part, cur.dtype),
            DMA((len(chunks),)),
            DMA((3,)),
            DMA((3,)),
            DMA((3,)),
            DMA((BLOCKS,)),
        ],
        compiler_params=params(),
        cost_estimate=LONG,
        name="own_rows",
    )(in_smem(table), *in_hbm(held), *chunks, prev, probes, cur, *after)


def final_kernel(factor, coded, prev, probes, cur, sums_in, _, out, sums, value, acc, sem):
    rows = prev.shape[1]
    scales = coded[pl.ds(BLOCKS * rows, 16), :].astype(jnp.int32).astype(jnp.float32)
    step = largest(scales[:8], scales[8:]) * (1.0 / LEVELS)
    for b in range(BLOCKS):
        image = coded[pl.ds(b * rows, rows), :].astype(jnp.int32).astype(jnp.float32) * step[b : b + 1]
        value[b] = 2.0 * image - prev[b]
    first = (1 - lax.axis_index("grp") // 2) * BLOCKS
    send = copy(value, out.at[pl.ds(first, BLOCKS)], sem)
    acc[...] = sums_in[...]
    for b in range(BLOCKS):
        add_sums(factor, value[b], probes[b], cur[b], acc)
    for n in range(2):
        sums[pl.ds(n, 1), :] = jnp.sum(acc[pl.ds(8 * n, 8), :], axis=0, keepdims=True)
    send.wait()


def other_rows(factor, coded, prev, probes, cur, t_next, sums):
    cols = cur.shape[2]
    return pl.pallas_call(
        functools.partial(final_kernel, factor),
        in_specs=[VMEM] * 5 + [HBM],
        out_specs=[HBM, VMEM],
        out_shape=[
            pltpu.HBM(t_next.shape, jnp.float32),
            jax.ShapeDtypeStruct((2, cols), jnp.float32),
        ],
        scratch_shapes=[pltpu.VMEM(prev.shape, jnp.float32), pltpu.VMEM((16, cols), jnp.float32), DMA],
        input_output_aliases={5: 0},
        compiler_params=params(),
        cost_estimate=LIGHT,
        name="other_rows",
    )(*in_vmem([coded, prev, probes, cur, sums]), *in_hbm([t_next]))


def gate(value, *after):
    return pl.pallas_call(
        lambda *refs: None,
        in_specs=[ANY] + [SMEM if a.dtype == jnp.int32 else ANY for a in after],
        out_specs=ANY,
        out_shape=jax.ShapeDtypeStruct(value.shape, value.dtype),
        input_output_aliases={0: 0},
        compiler_params=params(),
        cost_estimate=LIGHT,
        name="gate",
    )(value, *[in_smem(a) if a.dtype == jnp.int32 else a for a in after])


def sum_over(value, axis):
    size = lax.axis_size(axis)
    if size & (size - 1):
        return lax.psum(value, axis)
    hop = 1
    while hop < size:
        value = value + lax.ppermute(value, axis, [(i, i ^ hop) for i in range(size)])
        hop *= 2
    return value


def shards(tiles, neighbours, t_cur, t_prev, probes):
    blocks, rows, cols = t_cur.shape
    per = tiles.shape[0]
    slabs, lanes = lax.axis_size("slab"), lax.axis_size("grp")
    factor = 1.0 / math.sqrt(slabs * blocks * rows)
    across = functools.partial(lax.ppermute, axis_name="grp", perm=[(i, i ^ 2) for i in range(lanes)])
    sibling = functools.partial(lax.ppermute, axis_name="grp", perm=[(i, i ^ 1) for i in range(lanes)])
    pair = functools.partial(lax.ppermute, axis_name="slab", perm=[(i, i ^ 1) for i in range(slabs)])
    along = functools.partial(
        lax.ppermute,
        axis_name="slab",
        perm=[(i, (i + 2 if i % 2 == 0 else i - 2) % slabs) for i in range(slabs)],
    )

    tiles, t_prev, probes, fixed = in_hbm([tiles, t_prev, probes, t_cur])
    half = blocks // 2
    low, high = t_cur[:half], t_cur[half:]

    sib_tiles = sibling(tiles)
    oth = [across(low), across(high)]
    near_high = pair(high)
    table = meets(neighbours)
    held = [squares(tiles, rows, False)]
    held.append(squares(sib_tiles, rows, True))
    near_oth = [pair(gate(oth[0], held[0], table)), pair(oth[1])]
    far_high = along(near_high)
    far_oth = [along(near_oth[0]), across(far_high)]
    near_low = pair(gate(low, held[1]))
    far_low = across(far_oth[0])

    images = other_images(table, held, [*oth, *near_oth, *far_oth], ())
    images = gate(images, near_low, far_low)
    back = across(images)
    own = [fixed, near_low, near_high, far_low, far_high]
    t_next, sums, *later = own_rows(table, held, own, factor, t_prev, probes, fixed, in_hbm([images]))
    t_next, sums = other_rows(factor, back, *later, t_next, sums)
    return (t_next, sum_over(sums, "slab"))


def solution(mesh):
    placed = (
        P(("slab", "grp"), None, None),
        P("slab", None),
        P("slab", None, "grp"),
        P("slab", None, "grp"),
        P("slab", None, "grp"),
    )
    return jax.shard_map(
        shards,
        mesh=mesh,
        in_specs=placed,
        out_specs=(P("slab", None, "grp"), P(None, "grp")),
        check_vma=False,
    )
```

```python
import functools
import math

import jax
import jax.numpy as jnp
from jax import lax
from jax.experimental import pallas as pl
from jax.experimental.pallas import tpu as pltpu
from jax.sharding import PartitionSpec as P

GRANT = 20 * 1024 * 1024
BLOCKS = 6
TABLE = 8
PAD = 64
LEVELS = 32760.0
LIGHT = pl.CostEstimate(flops=1, bytes_accessed=1, transcendentals=0)
LONG = pl.CostEstimate(flops=1, bytes_accessed=1_000_000_000, transcendentals=0)
HEAVY = pl.CostEstimate(flops=1, bytes_accessed=18_000_000, transcendentals=0)
VMEM = pl.BlockSpec(memory_space=pltpu.VMEM)
SMEM = pl.BlockSpec(memory_space=pltpu.SMEM)
HBM = pl.BlockSpec(memory_space=pltpu.HBM)
ANY = pl.BlockSpec(memory_space=pl.ANY)
DMA = pltpu.SemaphoreType.DMA


def in_vmem(arrays):
    return [pltpu.with_memory_space_constraint(a, pltpu.VMEM) for a in arrays]


def in_smem(table):
    return pltpu.with_memory_space_constraint(table, pltpu.SMEM)


def in_hbm(arrays):
    return [pltpu.with_memory_space_constraint(a, pltpu.HBM) for a in arrays]


def params():
    return pltpu.CompilerParams(vmem_limit_bytes=GRANT)


def copy(src, dst, sem):
    made = pltpu.make_async_copy(src, dst, sem)
    made.start()
    return made


def order_kernel(neighbours, out, table, sem):
    blocks, neigh = neighbours.shape
    slab, lane = lax.axis_index("slab"), lax.axis_index("grp")
    per = BLOCKS // 2
    table[...] = jnp.zeros_like(table)
    for side, first in enumerate((lane * per, (lane ^ 1) * per)):
        for n in range(per):
            table[pl.ds(side * per + n, 1), :neigh] = neighbours[pl.ds(first + n, 1), :]
    mine = table[:TABLE, :]
    owner = mine // blocks
    spot = lax.broadcasted_iota(jnp.int32, mine.shape, 1)
    kind = jnp.where(owner == slab, 0, jnp.where(owner == (slab ^ 1), 1, 2))
    kind = jnp.where(spot < neigh, kind, 3)
    near = kind * blocks + mine - owner * blocks
    key = kind * 128 + spot
    slot = jnp.zeros_like(mine)
    for k in range(neigh):
        slot += (key[:, k : k + 1] < key).astype(jnp.int32)
    order = found = jnp.zeros_like(mine)
    for k in range(neigh):
        here = spot == k
        hit = slot == k
        order = jnp.where(here, jnp.sum(jnp.where(hit, spot, 0), axis=1, keepdims=True), order)
        found = jnp.where(here, jnp.sum(jnp.where(hit, near, 0), axis=1, keepdims=True), found)
    own = found < blocks
    count = jnp.sum((kind == 0).astype(jnp.int32), axis=1, keepdims=True)
    table[:TABLE, :] = order
    table[TABLE : 2 * TABLE, :] = jnp.where(own, found, blocks)
    table[2 * TABLE : 3 * TABLE, :] = jnp.where(own, 2 * blocks, found - blocks)
    table[3 * TABLE :, :] = jnp.broadcast_to(count, mine.shape)
    copy(table, out, sem).wait()


def ordered(neighbours):
    return pl.pallas_call(
        order_kernel,
        in_specs=[VMEM],
        out_specs=SMEM,
        out_shape=pltpu.SMEM((4 * TABLE, 128), jnp.int32),
        scratch_shapes=[pltpu.VMEM((4 * TABLE, 128), jnp.int32), DMA],
        compiler_params=params(),
        cost_estimate=LIGHT,
        name="ordered",
    )(neighbours)


def square_part(src, held, low):
    neigh, wide = src.shape[0], held.shape[2]
    piece = [src[:, pl.ds(pl.multiple_of(j * wide, wide), wide)] for j in range(16)]
    held[:, pl.ds(low, 16), :] = jnp.transpose(jnp.stack(piece, axis=0), (1, 0, 2))


def square_kernel(parts, tiles, held, raw, sems):
    count, _, half, wide = held.shape
    each = parts // count
    size = half // each
    loads = []
    for n in range(parts):
        src = tiles.at[n // each, :, pl.ds((n % each) * size * wide, size * wide)]
        loads.append(copy(src, raw.at[n], sems.at[n]))
    for n in range(parts):
        loads[n].wait()

        @pl.loop(0, size // 16)
        def _(step):
            low = pl.multiple_of((n % each) * size + step * 16, 16)
            src = raw.at[n, :, pl.ds(pl.multiple_of(step * 16 * wide, 128), 16 * wide)]
            square_part(src, held.at[n // each], low)


def held_kernel(tiles, held):
    count, _, half, wide = held.shape

    @pl.loop(0, count * (half // 16))
    def _(step):
        b, part = step // (half // 16), step % (half // 16)
        src = tiles.at[b, :, pl.ds(pl.multiple_of(part * 16 * wide, 128), 16 * wide)]
        square_part(src, held.at[b], pl.multiple_of(part * 16, 16))


def squares(tiles, rows, resident):
    count, neigh = tiles.shape[:2]
    half, wide = rows // 2, 2 * rows
    parts = 3 * count
    raw = [pltpu.VMEM((parts, neigh, rows * rows // 3), tiles.dtype), DMA((parts,))]
    return pl.pallas_call(
        held_kernel if resident else functools.partial(square_kernel, parts),
        in_specs=[VMEM if resident else HBM],
        out_specs=VMEM,
        out_shape=pltpu.VMEM((count, neigh, half, wide), tiles.dtype),
        scratch_shapes=[] if resident else raw,
        compiler_params=params(),
        cost_estimate=HEAVY,
        name="squares",
    )(*(in_vmem([tiles]) if resident else in_hbm([tiles])))


def start_near(sides, near, sems):
    copies = []
    cols = near.shape[2] // len(sides)
    for side, chunks in enumerate(sides):
        at = 0
        for chunk in chunks:
            spot = near.at[pl.ds(at, chunk.shape[0]), :, pl.ds(side * cols, cols)]
            copies.append(copy(chunk, spot, sems.at[len(copies)]))
            at += chunk.shape[0]
    near[near.shape[0] - 1] = jnp.zeros(near.shape[1:], near.dtype)
    return copies


def multiply(tiles, table, b, part, first, count, near):
    half, wide = tiles.shape[1:]
    rows = wide // 2
    lane = lax.broadcasted_iota(jnp.int32, (half, 128), 1)
    even = odd = None
    for k in range(first, first + count):
        vec = near[table[part * TABLE + b, k]]
        tile = tiles[table[b, k]]
        mid = tile[:, 128:256]
        none = jnp.zeros_like(mid)
        left = jnp.concatenate([tile[:, :128], jnp.where(lane < PAD, mid, none)], axis=1)
        right = jnp.concatenate([jnp.where(lane < PAD, none, mid), tile[:, 256:]], axis=1)
        one = jnp.concatenate([vec, vec[:PAD]], axis=0)
        two = jnp.concatenate([vec[rows - PAD :], vec], axis=0)
        one = jnp.dot(left, one, preferred_element_type=jnp.float32)
        two = jnp.dot(right, two, preferred_element_type=jnp.float32)
        even = one if even is None else even + one
        odd = two if odd is None else odd + two
    return even, odd


def each_block(held, body):
    first = 0
    for square in held:
        start = first

        @pl.loop(0, square.shape[0])
        def _(n):
            body(start + n, square.at[n])

        first += square.shape[0]


def any_block(needed):
    found = needed(0)
    for b in range(1, BLOCKS):
        found |= needed(b)
    return found


def place(b):
    per = BLOCKS // 2
    core = lax.axis_index("grp") % 2
    return jnp.where(b < per, core * per + b, (1 - core) * per + b - per)


def near_scratch(chunks, sides):
    rows, cols = chunks[0].shape[1:]
    return pltpu.VMEM((sum(c.shape[0] for c in chunks) + 1, rows, sides * cols), chunks[0].dtype)


def slab_kernel(n_other, table, first, second, own, *refs):
    other = refs[:n_other]
    acc, near, near_sems = refs[-3:]
    held = (first, second)
    for load in start_near(([own], other), near, near_sems):
        load.wait()

    def body(b, tiles):
        acc[b, 0], acc[b, 1] = multiply(tiles, table, b, 1, 0, 9, near)

    each_block(held, body)
    for group in range(1, 3):
        more = lambda b: table[3 * TABLE + b, 0] > 9 * group

        @pl.when(any_block(more))
        def _():
            def spread(b, tiles):
                @pl.when(more(b))
                def _():
                    even, odd = multiply(tiles, table, b, 1, 9 * group, 9, near)
                    acc[b, 0] += even
                    acc[b, 1] += odd

            each_block(held, spread)


def own_slab(table, held, own, other):
    cols = own.shape[2]
    return pl.pallas_call(
        functools.partial(slab_kernel, len(other)),
        in_specs=[SMEM] + [VMEM] * 2 + [ANY] * (1 + len(other)),
        out_specs=VMEM,
        out_shape=pltpu.VMEM((BLOCKS, 2, held[0].shape[2], 2 * cols), jnp.float32),
        scratch_shapes=[near_scratch([own], 2), DMA((1 + len(other),))],
        compiler_params=params(),
        cost_estimate=LIGHT,
        name="own_slab",
    )(in_smem(table), *in_vmem(held), own, *other)


def largest(power, size):
    return size * jnp.exp2(power - 14.0)


def few(table):
    return lambda b: table[3 * TABLE + b, 0] < 9


def other_kernel(n_chunks, table, acc, first, second, *refs):
    chunks = refs[:n_chunks]
    out, near, total, image, scales, near_sems = refs[-6:]
    half, rows, cols = first.shape[2], image.shape[0], image.shape[1]
    scales[...] = jnp.zeros_like(scales)
    loads = start_near((chunks,), near, near_sems)
    for n in range(2):
        for b in range(BLOCKS):
            total[b, n] = acc[b, n, :, cols:]
    for load in loads:
        load.wait()

    @pl.when(any_block(few(table)))
    def _():
        def spread(b, tiles):
            @pl.when(few(table)(b))
            def _():
                even, odd = multiply(tiles, table, b, 2, 0, 9, near)
                total[b, 0] += even
                total[b, 1] += odd

        each_block((first, second), spread)

    def body(b, tiles):
        even, odd = multiply(tiles, table, b, 2, 9, 18, near)
        image[pl.ds(0, half, 2), :] = total[b, 0] + even
        image[pl.ds(1, half, 2), :] = total[b, 1] + odd
        value = image[...]
        top = jnp.maximum(jnp.max(jnp.abs(value), axis=0, keepdims=True), 1e-30)
        power = jnp.ceil(jnp.log2(top))
        size = jnp.ceil(top * jnp.exp2(14.0 - power))
        scales[pl.ds(place(b), 1), :] = power
        scales[pl.ds(8 + place(b), 1), :] = size
        value = jnp.round(value * (LEVELS / largest(power, size)))
        rows_out = pl.ds(pl.multiple_of(place(b) * rows, rows), rows)
        out[rows_out, :] = value.astype(jnp.int32).astype(jnp.int16)

    each_block((first, second), body)
    out[pl.ds(BLOCKS * rows, 16), :] = scales[...].astype(jnp.int32).astype(jnp.int16)


def other_images(table, acc, held, chunks, after):
    rows, cols = chunks[0].shape[1:]
    return pl.pallas_call(
        functools.partial(other_kernel, len(chunks)),
        in_specs=[SMEM] + [VMEM] * 3 + [ANY] * (len(chunks) + len(after)),
        out_specs=VMEM,
        out_shape=pltpu.VMEM((BLOCKS * rows + 16, cols), jnp.int16),
        scratch_shapes=[
            near_scratch(chunks, 1),
            pltpu.VMEM((BLOCKS, 2, rows // 2, cols), jnp.float32),
            pltpu.VMEM((rows, cols), jnp.float32),
            pltpu.VMEM((16, cols), jnp.float32),
            DMA((len(chunks),)),
        ],
        compiler_params=params(),
        cost_estimate=LONG,
        name="other_images",
    )(in_smem(table), *in_vmem([acc, *held]), *chunks, *after)


def add_sums(factor, value, probes, cur, sums):
    for n, term in enumerate((probes * value, cur.astype(jnp.float32) * value)):
        part = jnp.sum(term.reshape(-1, 8, term.shape[-1]), axis=0) * factor
        sums[pl.ds(8 * n, 8), :] += part


def own_kernel(n_chunks, factor, table, acc, first_held, second_held, *refs):
    chunks, rows_in = refs[:n_chunks], refs[n_chunks : n_chunks + 3]
    out, sums, *later = refs[n_chunks + 4 : n_chunks + 9]
    near, image, prev, probes, cur, near_sems, row_sems, later_sems, out_sems = refs[-9:]
    half = first_held.shape[2]
    loads = start_near((chunks,), near, near_sems)
    cols = image.shape[2]
    first = (lax.axis_index("grp") // 2) * BLOCKS
    mine = []
    for n, (src, dst) in enumerate(zip(rows_in, (prev, probes, cur))):
        mine.append(copy(src.at[pl.ds(first, BLOCKS)], dst, row_sems.at[n]))
    sums[...] = jnp.zeros_like(sums)
    for made in loads:
        made.wait()

    def body(b, tiles):
        at = place(b)
        even, odd = multiply(tiles, table, b, 2, 9, 18, near)
        image[b, pl.ds(0, half, 2), :] = acc[b, 0, :, :cols] + even
        image[b, pl.ds(1, half, 2), :] = acc[b, 1, :, :cols] + odd

        @pl.when(few(table)(b))
        def _():
            even, odd = multiply(tiles, table, b, 2, 0, 9, near)
            image[b, pl.ds(0, half, 2), :] += even
            image[b, pl.ds(1, half, 2), :] += odd

        @pl.when(b == 0)
        def _():
            for made in mine:
                made.wait()
            for n, (src, dst) in enumerate(zip(rows_in, later)):
                copy(src.at[pl.ds(BLOCKS - first, BLOCKS)], dst, later_sems.at[n])

        value = 2.0 * image[b] - prev[at]
        image[b] = value
        copy(image.at[b], out.at[first + at], out_sems.at[b])
        add_sums(factor, value, probes[at], cur[at], sums)

    each_block((first_held, second_held), body)
    for n, (src, dst) in enumerate(zip(rows_in, later)):
        pltpu.make_async_copy(src.at[pl.ds(BLOCKS - first, BLOCKS)], dst, later_sems.at[n]).wait()
    for b in range(BLOCKS):
        pltpu.make_async_copy(image.at[b], out.at[first + place(b)], out_sems.at[b]).wait()


def own_rows(table, acc, held, chunks, factor, prev, probes, cur, after):
    rows, cols = cur.shape[1:]
    part = (BLOCKS, rows, cols)
    return pl.pallas_call(
        functools.partial(own_kernel, len(chunks), factor),
        in_specs=[SMEM] + [VMEM] * 3 + [ANY] * (len(chunks) + 3 + len(after)),
        out_specs=[HBM] + [VMEM] * 4,
        out_shape=[
            pltpu.HBM(prev.shape, jnp.float32),
            pltpu.VMEM((16, cols), jnp.float32),
            pltpu.VMEM(part, jnp.float32),
            pltpu.VMEM(part, jnp.float32),
            pltpu.VMEM(part, cur.dtype),
        ],
        scratch_shapes=[
            near_scratch(chunks, 1),
            pltpu.VMEM(part, jnp.float32),
            pltpu.VMEM(part, jnp.float32),
            pltpu.VMEM(part, jnp.float32),
            pltpu.VMEM(part, cur.dtype),
            DMA((len(chunks),)),
            DMA((3,)),
            DMA((3,)),
            DMA((BLOCKS,)),
        ],
        compiler_params=params(),
        cost_estimate=LONG,
        name="own_rows",
    )(in_smem(table), *in_vmem([acc, *held]), *chunks, prev, probes, cur, *after)


def final_kernel(factor, coded, prev, probes, cur, sums_in, _, out, sums, value, acc, sem):
    rows = prev.shape[1]
    scales = coded[pl.ds(BLOCKS * rows, 16), :].astype(jnp.int32).astype(jnp.float32)
    step = largest(scales[:8], scales[8:]) * (1.0 / LEVELS)
    for b in range(BLOCKS):
        image = coded[pl.ds(b * rows, rows), :].astype(jnp.int32).astype(jnp.float32) * step[b : b + 1]
        value[b] = 2.0 * image - prev[b]
    first = (1 - lax.axis_index("grp") // 2) * BLOCKS
    send = copy(value, out.at[pl.ds(first, BLOCKS)], sem)
    acc[...] = sums_in[...]
    for b in range(BLOCKS):
        add_sums(factor, value[b], probes[b], cur[b], acc)
    for n in range(2):
        sums[pl.ds(n, 1), :] = jnp.sum(acc[pl.ds(8 * n, 8), :], axis=0, keepdims=True)
    send.wait()


def other_rows(factor, coded, prev, probes, cur, t_next, sums):
    cols = cur.shape[2]
    return pl.pallas_call(
        functools.partial(final_kernel, factor),
        in_specs=[VMEM] * 5 + [HBM],
        out_specs=[HBM, VMEM],
        out_shape=[
            pltpu.HBM(t_next.shape, jnp.float32),
            jax.ShapeDtypeStruct((2, cols), jnp.float32),
        ],
        scratch_shapes=[pltpu.VMEM(prev.shape, jnp.float32), pltpu.VMEM((16, cols), jnp.float32), DMA],
        input_output_aliases={5: 0},
        compiler_params=params(),
        cost_estimate=LIGHT,
        name="other_rows",
    )(*in_vmem([coded, prev, probes, cur, sums]), *in_hbm([t_next]))


def gate(value, *after):
    return pl.pallas_call(
        lambda *refs: None,
        in_specs=[ANY] + [SMEM if a.dtype == jnp.int32 else ANY for a in after],
        out_specs=ANY,
        out_shape=jax.ShapeDtypeStruct(value.shape, value.dtype),
        input_output_aliases={0: 0},
        compiler_params=params(),
        cost_estimate=LIGHT,
        name="gate",
    )(value, *[in_smem(a) if a.dtype == jnp.int32 else a for a in after])


def sum_over(value, axis):
    size = lax.axis_size(axis)
    if size & (size - 1):
        return lax.psum(value, axis)
    hop = 1
    while hop < size:
        value = value + lax.ppermute(value, axis, [(i, i ^ hop) for i in range(size)])
        hop *= 2
    return value


def shards(tiles, neighbours, t_cur, t_prev, probes):
    blocks, rows, cols = t_cur.shape
    per = tiles.shape[0]
    slabs, lanes = lax.axis_size("slab"), lax.axis_size("grp")
    factor = 1.0 / math.sqrt(slabs * blocks * rows)
    across = functools.partial(lax.ppermute, axis_name="grp", perm=[(i, i ^ 2) for i in range(lanes)])
    sibling = functools.partial(lax.ppermute, axis_name="grp", perm=[(i, i ^ 1) for i in range(lanes)])
    pair = functools.partial(lax.ppermute, axis_name="slab", perm=[(i, i ^ 1) for i in range(slabs)])
    along = functools.partial(
        lax.ppermute,
        axis_name="slab",
        perm=[(i, (i + 2 if i % 2 == 0 else i - 2) % slabs) for i in range(slabs)],
    )

    tiles, t_prev, probes, fixed = in_hbm([tiles, t_prev, probes, t_cur])
    half = blocks // 2
    low, high = t_cur[:half], t_cur[half:]

    sib_tiles = sibling(tiles)
    oth = [across(low), across(high)]
    near_high = pair(high)
    table = ordered(neighbours)
    held = [squares(tiles, rows, False), squares(sib_tiles, rows, True)]
    oth[0] = gate(oth[0], held[0], table)
    near_oth = [pair(c) for c in oth]
    far_high = along(near_high)
    far_oth = [along(near_oth[0]), across(far_high)]
    acc = own_slab(table, held, fixed, oth)
    near_low = pair(gate(low, acc))
    far_low = across(far_oth[0])

    images = other_images(table, acc, held, [*near_oth, *far_oth], ())
    images = gate(images, near_low, far_low)
    back = across(images)
    own = [near_low, near_high, far_low, far_high]
    t_next, sums, *later = own_rows(table, acc, held, own, factor, t_prev, probes, fixed, [images])
    t_next, sums = other_rows(factor, back, *later, t_next, sums)
    return (t_next, sum_over(sums, "slab"))


def solution(mesh):
    placed = (
        P(("slab", "grp"), None, None),
        P("slab", None),
        P("slab", None, "grp"),
        P("slab", None, "grp"),
        P("slab", None, "grp"),
    )
    return jax.shard_map(
        shards,
        mesh=mesh,
        in_specs=placed,
        out_specs=(P("slab", None, "grp"), P(None, "grp")),
        check_vma=False,
    )
```

```python
import functools
import math

import jax
import jax.numpy as jnp
from jax import lax
from jax.experimental import pallas as pl
from jax.experimental.pallas import tpu as pltpu
from jax.sharding import PartitionSpec as P

GRANT = 20 * 1024 * 1024
BLOCKS = 6
TABLE = 8
PAD = 64
LEVELS = 32760.0
LIGHT = pl.CostEstimate(flops=1, bytes_accessed=1, transcendentals=0)
LONG = pl.CostEstimate(flops=1, bytes_accessed=1_000_000_000, transcendentals=0)
HEAVY = pl.CostEstimate(flops=1, bytes_accessed=18_000_000, transcendentals=0)
VMEM = pl.BlockSpec(memory_space=pltpu.VMEM)
SMEM = pl.BlockSpec(memory_space=pltpu.SMEM)
HBM = pl.BlockSpec(memory_space=pltpu.HBM)
ANY = pl.BlockSpec(memory_space=pl.ANY)
DMA = pltpu.SemaphoreType.DMA


def in_vmem(arrays):
    return [pltpu.with_memory_space_constraint(a, pltpu.VMEM) for a in arrays]


def in_smem(table):
    return pltpu.with_memory_space_constraint(table, pltpu.SMEM)


def in_hbm(arrays):
    return [pltpu.with_memory_space_constraint(a, pltpu.HBM) for a in arrays]


def params():
    return pltpu.CompilerParams(vmem_limit_bytes=GRANT)


def copy(src, dst, sem):
    made = pltpu.make_async_copy(src, dst, sem)
    made.start()
    return made


def order_kernel(neighbours, out, table, sem):
    blocks, neigh = neighbours.shape
    slab, lane = lax.axis_index("slab"), lax.axis_index("grp")
    per = BLOCKS // 2
    table[...] = jnp.zeros_like(table)
    for side, first in enumerate((lane * per, (lane ^ 1) * per)):
        for n in range(per):
            table[pl.ds(side * per + n, 1), :neigh] = neighbours[pl.ds(first + n, 1), :]
    mine = table[:TABLE, :]
    owner = mine // blocks
    spot = lax.broadcasted_iota(jnp.int32, mine.shape, 1)
    kind = jnp.where(owner == slab, 0, jnp.where(owner == (slab ^ 1), 1, 2))
    kind = jnp.where(spot < neigh, kind, 3)
    near = kind * blocks + mine - owner * blocks
    key = kind * 128 + spot
    slot = jnp.zeros_like(mine)
    for k in range(neigh):
        slot += (key[:, k : k + 1] < key).astype(jnp.int32)
    order = found = jnp.zeros_like(mine)
    for k in range(neigh):
        here = spot == k
        hit = slot == k
        order = jnp.where(here, jnp.sum(jnp.where(hit, spot, 0), axis=1, keepdims=True), order)
        found = jnp.where(here, jnp.sum(jnp.where(hit, near, 0), axis=1, keepdims=True), found)
    own = found < blocks
    count = jnp.sum((kind == 0).astype(jnp.int32), axis=1, keepdims=True)
    table[:TABLE, :] = order
    table[TABLE : 2 * TABLE, :] = jnp.where(own, found, blocks)
    table[2 * TABLE : 3 * TABLE, :] = jnp.where(own, 2 * blocks, found - blocks)
    table[3 * TABLE :, :] = jnp.broadcast_to(count, mine.shape)
    copy(table, out, sem).wait()


def ordered(neighbours):
    return pl.pallas_call(
        order_kernel,
        in_specs=[VMEM],
        out_specs=SMEM,
        out_shape=pltpu.SMEM((4 * TABLE, 128), jnp.int32),
        scratch_shapes=[pltpu.VMEM((4 * TABLE, 128), jnp.int32), DMA],
        compiler_params=params(),
        cost_estimate=LIGHT,
        name="ordered",
    )(neighbours)


def square_part(src, held, low):
    neigh, wide = src.shape[0], held.shape[2]
    piece = [src[:, pl.ds(pl.multiple_of(j * wide, wide), wide)] for j in range(16)]
    held[:, pl.ds(low, 16), :] = jnp.transpose(jnp.stack(piece, axis=0), (1, 0, 2))


def square_kernel(parts, tiles, held, raw, sems):
    count, _, half, wide = held.shape
    each = parts // count
    size = half // each
    loads = []
    for n in range(parts):
        src = tiles.at[n // each, :, pl.ds((n % each) * size * wide, size * wide)]
        loads.append(copy(src, raw.at[n], sems.at[n]))
    for n in range(parts):
        loads[n].wait()

        @pl.loop(0, size // 16)
        def _(step):
            low = pl.multiple_of((n % each) * size + step * 16, 16)
            src = raw.at[n, :, pl.ds(pl.multiple_of(step * 16 * wide, 128), 16 * wide)]
            square_part(src, held.at[n // each], low)


def held_kernel(tiles, held):
    count, _, half, wide = held.shape

    @pl.loop(0, count * (half // 16))
    def _(step):
        b, part = step // (half // 16), step % (half // 16)
        src = tiles.at[b, :, pl.ds(pl.multiple_of(part * 16 * wide, 128), 16 * wide)]
        square_part(src, held.at[b], pl.multiple_of(part * 16, 16))


def squares(tiles, rows, resident):
    count, neigh = tiles.shape[:2]
    half, wide = rows // 2, 2 * rows
    parts = 3 * count
    raw = [pltpu.VMEM((parts, neigh, rows * rows // 3), tiles.dtype), DMA((parts,))]
    return pl.pallas_call(
        held_kernel if resident else functools.partial(square_kernel, parts),
        in_specs=[VMEM if resident else HBM],
        out_specs=VMEM,
        out_shape=pltpu.VMEM((count, neigh, half, wide), tiles.dtype),
        scratch_shapes=[] if resident else raw,
        compiler_params=params(),
        cost_estimate=HEAVY,
        name="squares",
    )(*(in_vmem([tiles]) if resident else in_hbm([tiles])))


def start_near(sides, near, sems):
    copies = []
    cols = near.shape[2] // len(sides)
    for side, chunks in enumerate(sides):
        at = 0
        for chunk in chunks:
            spot = near.at[pl.ds(at, chunk.shape[0]), :, pl.ds(side * cols, cols)]
            copies.append(copy(chunk, spot, sems.at[len(copies)]))
            at += chunk.shape[0]
    near[near.shape[0] - 1] = jnp.zeros(near.shape[1:], near.dtype)
    return copies


def multiply(tiles, table, b, part, first, count, near):
    half, wide = tiles.shape[1:]
    rows = wide // 2
    lane = lax.broadcasted_iota(jnp.int32, (half, 128), 1)
    even = odd = None
    for k in range(first, first + count):
        vec = near[table[part * TABLE + b, k]]
        tile = tiles[table[b, k]]
        mid = tile[:, 128:256]
        none = jnp.zeros_like(mid)
        left = jnp.concatenate([tile[:, :128], jnp.where(lane < PAD, mid, none)], axis=1)
        right = jnp.concatenate([jnp.where(lane < PAD, none, mid), tile[:, 256:]], axis=1)
        one = jnp.concatenate([vec, vec[:PAD]], axis=0)
        two = jnp.concatenate([vec[rows - PAD :], vec], axis=0)
        one = jnp.dot(left, one, preferred_element_type=jnp.float32)
        two = jnp.dot(right, two, preferred_element_type=jnp.float32)
        even = one if even is None else even + one
        odd = two if odd is None else odd + two
    return even, odd


def each_block(held, body):
    first = 0
    for square in held:
        start = first

        @pl.loop(0, square.shape[0])
        def _(n):
            body(start + n, square.at[n])

        first += square.shape[0]


def any_block(needed):
    found = needed(0)
    for b in range(1, BLOCKS):
        found |= needed(b)
    return found


def place(b):
    per = BLOCKS // 2
    core = lax.axis_index("grp") % 2
    return jnp.where(b < per, core * per + b, (1 - core) * per + b - per)


def near_scratch(chunks, sides):
    rows, cols = chunks[0].shape[1:]
    return pltpu.VMEM((sum(c.shape[0] for c in chunks) + 1, rows, sides * cols), chunks[0].dtype)


def slab_kernel(n_other, table, first, second, own, *refs):
    other = refs[:n_other]
    acc, near, near_sems = refs[-3:]
    held = (first, second)
    for load in start_near(([own], other), near, near_sems):
        load.wait()

    def body(b, tiles):
        acc[b, 0], acc[b, 1] = multiply(tiles, table, b, 1, 0, 9, near)

    each_block(held, body)
    for group in range(1, 3):
        more = lambda b: table[3 * TABLE + b, 0] > 9 * group

        @pl.when(any_block(more))
        def _():
            def spread(b, tiles):
                @pl.when(more(b))
                def _():
                    even, odd = multiply(tiles, table, b, 1, 9 * group, 9, near)
                    acc[b, 0] += even
                    acc[b, 1] += odd

            each_block(held, spread)


def own_slab(table, held, own, other):
    cols = own.shape[2]
    return pl.pallas_call(
        functools.partial(slab_kernel, len(other)),
        in_specs=[SMEM] + [VMEM] * 2 + [ANY] * (1 + len(other)),
        out_specs=VMEM,
        out_shape=pltpu.VMEM((BLOCKS, 2, held[0].shape[2], 2 * cols), jnp.float32),
        scratch_shapes=[near_scratch([own], 2), DMA((1 + len(other),))],
        compiler_params=params(),
        cost_estimate=LIGHT,
        name="own_slab",
    )(in_smem(table), *in_vmem(held), own, *other)


def largest(power, size):
    return size * jnp.exp2(power - 14.0)


def few(table):
    return lambda b: table[3 * TABLE + b, 0] < 9


def other_kernel(n_chunks, table, acc, first, second, *refs):
    chunks = refs[:n_chunks]
    out, near, total, image, scales, near_sems = refs[-6:]
    half, rows, cols = first.shape[2], image.shape[0], image.shape[1]
    scales[...] = jnp.zeros_like(scales)
    loads = start_near((chunks,), near, near_sems)
    for n in range(2):
        for b in range(BLOCKS):
            total[b, n] = acc[b, n, :, cols:]
    for load in loads:
        load.wait()

    @pl.when(any_block(few(table)))
    def _():
        def spread(b, tiles):
            @pl.when(few(table)(b))
            def _():
                even, odd = multiply(tiles, table, b, 2, 0, 9, near)
                total[b, 0] += even
                total[b, 1] += odd

        each_block((first, second), spread)

    def body(b, tiles):
        even, odd = multiply(tiles, table, b, 2, 9, 18, near)
        image[pl.ds(0, half, 2), :] = total[b, 0] + even
        image[pl.ds(1, half, 2), :] = total[b, 1] + odd
        value = image[...]
        top = jnp.maximum(jnp.max(jnp.abs(value), axis=0, keepdims=True), 1e-30)
        power = jnp.ceil(jnp.log2(top))
        size = jnp.ceil(top * jnp.exp2(14.0 - power))
        scales[pl.ds(place(b), 1), :] = power
        scales[pl.ds(8 + place(b), 1), :] = size
        value = jnp.round(value * (LEVELS / largest(power, size)))
        rows_out = pl.ds(pl.multiple_of(place(b) * rows, rows), rows)
        out[rows_out, :] = value.astype(jnp.int32).astype(jnp.int16)

    each_block((first, second), body)
    out[pl.ds(BLOCKS * rows, 16), :] = scales[...].astype(jnp.int32).astype(jnp.int16)


def other_images(table, acc, held, chunks, after):
    rows, cols = chunks[0].shape[1:]
    return pl.pallas_call(
        functools.partial(other_kernel, len(chunks)),
        in_specs=[SMEM] + [VMEM] * 3 + [ANY] * (len(chunks) + len(after)),
        out_specs=VMEM,
        out_shape=pltpu.VMEM((BLOCKS * rows + 16, cols), jnp.int16),
        scratch_shapes=[
            near_scratch(chunks, 1),
            pltpu.VMEM((BLOCKS, 2, rows // 2, cols), jnp.float32),
            pltpu.VMEM((rows, cols), jnp.float32),
            pltpu.VMEM((16, cols), jnp.float32),
            DMA((len(chunks),)),
        ],
        compiler_params=params(),
        cost_estimate=LONG,
        name="other_images",
    )(in_smem(table), *in_vmem([acc, *held]), *chunks, *after)


def add_sums(factor, value, probes, cur, sums):
    for n, term in enumerate((probes * value, cur.astype(jnp.float32) * value)):
        part = jnp.sum(term.reshape(-1, 8, term.shape[-1]), axis=0) * factor
        sums[pl.ds(8 * n, 8), :] += part


def own_kernel(n_chunks, factor, table, acc, first_held, second_held, *refs):
    chunks, rows_in = refs[:n_chunks], refs[n_chunks : n_chunks + 3]
    out, sums, *later = refs[n_chunks + 4 : n_chunks + 9]
    near, image, prev, probes, cur, near_sems, row_sems, later_sems, out_sems = refs[-9:]
    half = first_held.shape[2]
    loads = start_near((chunks,), near, near_sems)
    cols = image.shape[2]
    first = (lax.axis_index("grp") // 2) * BLOCKS
    mine = []
    for n, (src, dst) in enumerate(zip(rows_in, (prev, probes, cur))):
        mine.append(copy(src.at[pl.ds(first, BLOCKS)], dst, row_sems.at[n]))
    sums[...] = jnp.zeros_like(sums)
    for made in loads:
        made.wait()

    def body(b, tiles):
        at = place(b)
        even, odd = multiply(tiles, table, b, 2, 9, 18, near)
        image[b, pl.ds(0, half, 2), :] = acc[b, 0, :, :cols] + even
        image[b, pl.ds(1, half, 2), :] = acc[b, 1, :, :cols] + odd

        @pl.when(few(table)(b))
        def _():
            even, odd = multiply(tiles, table, b, 2, 0, 9, near)
            image[b, pl.ds(0, half, 2), :] += even
            image[b, pl.ds(1, half, 2), :] += odd

        @pl.when(b == 0)
        def _():
            for made in mine:
                made.wait()
            for n, (src, dst) in enumerate(zip(rows_in, later)):
                copy(src.at[pl.ds(BLOCKS - first, BLOCKS)], dst, later_sems.at[n])

        value = 2.0 * image[b] - prev[at]
        image[b] = value
        copy(image.at[b], out.at[first + at], out_sems.at[b])
        add_sums(factor, value, probes[at], cur[at], sums)

    each_block((first_held, second_held), body)
    for n, (src, dst) in enumerate(zip(rows_in, later)):
        pltpu.make_async_copy(src.at[pl.ds(BLOCKS - first, BLOCKS)], dst, later_sems.at[n]).wait()
    for b in range(BLOCKS):
        pltpu.make_async_copy(image.at[b], out.at[first + place(b)], out_sems.at[b]).wait()


def own_rows(table, acc, held, chunks, factor, prev, probes, cur, after):
    rows, cols = cur.shape[1:]
    part = (BLOCKS, rows, cols)
    return pl.pallas_call(
        functools.partial(own_kernel, len(chunks), factor),
        in_specs=[SMEM] + [VMEM] * 3 + [ANY] * (len(chunks) + 3 + len(after)),
        out_specs=[HBM] + [VMEM] * 4,
        out_shape=[
            pltpu.HBM(prev.shape, jnp.float32),
            pltpu.VMEM((16, cols), jnp.float32),
            pltpu.VMEM(part, jnp.float32),
            pltpu.VMEM(part, jnp.float32),
            pltpu.VMEM(part, cur.dtype),
        ],
        scratch_shapes=[
            near_scratch(chunks, 1),
            pltpu.VMEM(part, jnp.float32),
            pltpu.VMEM(part, jnp.float32),
            pltpu.VMEM(part, jnp.float32),
            pltpu.VMEM(part, cur.dtype),
            DMA((len(chunks),)),
            DMA((3,)),
            DMA((3,)),
            DMA((BLOCKS,)),
        ],
        compiler_params=params(),
        cost_estimate=LONG,
        name="own_rows",
    )(in_smem(table), *in_vmem([acc, *held]), *chunks, prev, probes, cur, *after)


def final_kernel(factor, coded, prev, probes, cur, sums_in, _, out, sums, value, acc, sem):
    rows = prev.shape[1]
    scales = coded[pl.ds(BLOCKS * rows, 16), :].astype(jnp.int32).astype(jnp.float32)
    step = largest(scales[:8], scales[8:]) * (1.0 / LEVELS)
    for b in range(BLOCKS):
        image = coded[pl.ds(b * rows, rows), :].astype(jnp.int32).astype(jnp.float32) * step[b : b + 1]
        value[b] = 2.0 * image - prev[b]
    first = (1 - lax.axis_index("grp") // 2) * BLOCKS
    send = copy(value, out.at[pl.ds(first, BLOCKS)], sem)
    acc[...] = sums_in[...]
    for b in range(BLOCKS):
        add_sums(factor, value[b], probes[b], cur[b], acc)
    for n in range(2):
        sums[pl.ds(n, 1), :] = jnp.sum(acc[pl.ds(8 * n, 8), :], axis=0, keepdims=True)
    send.wait()


def other_rows(factor, coded, prev, probes, cur, t_next, sums):
    cols = cur.shape[2]
    return pl.pallas_call(
        functools.partial(final_kernel, factor),
        in_specs=[VMEM] * 5 + [HBM],
        out_specs=[HBM, VMEM],
        out_shape=[
            pltpu.HBM(t_next.shape, jnp.float32),
            jax.ShapeDtypeStruct((2, cols), jnp.float32),
        ],
        scratch_shapes=[pltpu.VMEM(prev.shape, jnp.float32), pltpu.VMEM((16, cols), jnp.float32), DMA],
        input_output_aliases={5: 0},
        compiler_params=params(),
        cost_estimate=LIGHT,
        name="other_rows",
    )(*in_vmem([coded, prev, probes, cur, sums]), *in_hbm([t_next]))


def gate(value, *after):
    return pl.pallas_call(
        lambda *refs: None,
        in_specs=[ANY] + [SMEM if a.dtype == jnp.int32 else ANY for a in after],
        out_specs=ANY,
        out_shape=jax.ShapeDtypeStruct(value.shape, value.dtype),
        input_output_aliases={0: 0},
        compiler_params=params(),
        cost_estimate=LIGHT,
        name="gate",
    )(value, *[in_smem(a) if a.dtype == jnp.int32 else a for a in after])


def sum_over(value, axis):
    size = lax.axis_size(axis)
    if size & (size - 1):
        return lax.psum(value, axis)
    value, hop = value + lax.ppermute(value, axis, [(i, i ^ 1) for i in range(size)]), 2
    while hop < size:
        jumps = (hop, 2 * hop, 3 * hop) if 2 * hop < size else (hop,)
        far = [lax.ppermute(value, axis, [(i, i ^ j) for i in range(size)]) for j in jumps]
        value = value + far[0]
        if len(far) > 1:
            value = value + (far[1] + far[2])
        hop *= len(jumps) + 1
    return value


def shards(tiles, neighbours, t_cur, t_prev, probes):
    blocks, rows, cols = t_cur.shape
    per = tiles.shape[0]
    slabs, lanes = lax.axis_size("slab"), lax.axis_size("grp")
    factor = 1.0 / math.sqrt(slabs * blocks * rows)
    across = functools.partial(lax.ppermute, axis_name="grp", perm=[(i, i ^ 2) for i in range(lanes)])
    sibling = functools.partial(lax.ppermute, axis_name="grp", perm=[(i, i ^ 1) for i in range(lanes)])
    pair = functools.partial(lax.ppermute, axis_name="slab", perm=[(i, i ^ 1) for i in range(slabs)])
    along = functools.partial(
        lax.ppermute,
        axis_name="slab",
        perm=[(i, (i + 2 if i % 2 == 0 else i - 2) % slabs) for i in range(slabs)],
    )

    tiles, t_prev, probes, fixed = in_hbm([tiles, t_prev, probes, t_cur])
    half = blocks // 2
    low, high = t_cur[:half], t_cur[half:]

    sib_tiles = sibling(tiles)
    oth = [across(low), across(high)]
    near_high = pair(high)
    table = ordered(neighbours)
    held = [squares(tiles, rows, False), squares(sib_tiles, rows, True)]
    oth[0] = gate(oth[0], held[0], table)
    near_oth = [pair(oth[0]), pair(oth[1])]
    far_high = along(near_high)
    far_oth = [along(near_oth[0]), across(far_high)]
    acc = own_slab(table, held, fixed, oth)
    near_low = pair(gate(low, acc))
    far_low = across(far_oth[0])

    images = other_images(table, acc, held, [*near_oth, *far_oth], ())
    images = gate(images, near_low, far_low)
    back = across(images)
    own = [near_low, near_high, far_low, far_high]
    t_next, sums, *later = own_rows(table, acc, held, own, factor, t_prev, probes, fixed, [images])
    t_next, sums = other_rows(factor, back, *later, t_next, sums)
    return (t_next, sum_over(sums, "slab"))


def solution(mesh):
    placed = (
        P(("slab", "grp"), None, None),
        P("slab", None),
        P("slab", None, "grp"),
        P("slab", None, "grp"),
        P("slab", None, "grp"),
    )
    return jax.shard_map(
        shards,
        mesh=mesh,
        in_specs=placed,
        out_specs=(P("slab", None, "grp"), P(None, "grp")),
        check_vma=False,
    )
```

```python
import functools
import math

import jax
import jax.numpy as jnp
from jax import lax
from jax.experimental import pallas as pl
from jax.experimental.pallas import tpu as pltpu
from jax.sharding import PartitionSpec as P

GRANT = 20 * 1024 * 1024
BLOCKS = 6
TABLE = 8
PAD = 64
LEVELS = 32760.0
LIGHT = pl.CostEstimate(flops=1, bytes_accessed=1, transcendentals=0)
LONG = pl.CostEstimate(flops=1, bytes_accessed=1_000_000_000, transcendentals=0)
HEAVY = pl.CostEstimate(flops=1, bytes_accessed=18_000_000, transcendentals=0)
VMEM = pl.BlockSpec(memory_space=pltpu.VMEM)
SMEM = pl.BlockSpec(memory_space=pltpu.SMEM)
HBM = pl.BlockSpec(memory_space=pltpu.HBM)
ANY = pl.BlockSpec(memory_space=pl.ANY)
DMA = pltpu.SemaphoreType.DMA


def in_vmem(arrays):
    return [pltpu.with_memory_space_constraint(a, pltpu.VMEM) for a in arrays]


def in_smem(table):
    return pltpu.with_memory_space_constraint(table, pltpu.SMEM)


def in_hbm(arrays):
    return [pltpu.with_memory_space_constraint(a, pltpu.HBM) for a in arrays]


def params():
    return pltpu.CompilerParams(vmem_limit_bytes=GRANT)


def copy(src, dst, sem):
    made = pltpu.make_async_copy(src, dst, sem)
    made.start()
    return made


def order_kernel(neighbours, out, table, sem):
    blocks, neigh = neighbours.shape
    slab, lane = lax.axis_index("slab"), lax.axis_index("grp")
    per = BLOCKS // 2
    table[...] = jnp.zeros_like(table)
    for side, first in enumerate((lane * per, (lane ^ 1) * per)):
        for n in range(per):
            table[pl.ds(side * per + n, 1), :neigh] = neighbours[pl.ds(first + n, 1), :]
    mine = table[:TABLE, :]
    owner = mine // blocks
    spot = lax.broadcasted_iota(jnp.int32, mine.shape, 1)
    kind = jnp.where(owner == slab, 0, jnp.where(owner == (slab ^ 1), 1, 2))
    kind = jnp.where(spot < neigh, kind, 3)
    near = kind * blocks + mine - owner * blocks
    key = kind * 128 + spot
    slot = jnp.zeros_like(mine)
    for k in range(neigh):
        slot += (key[:, k : k + 1] < key).astype(jnp.int32)
    order = found = jnp.zeros_like(mine)
    for k in range(neigh):
        here = spot == k
        hit = slot == k
        order = jnp.where(here, jnp.sum(jnp.where(hit, spot, 0), axis=1, keepdims=True), order)
        found = jnp.where(here, jnp.sum(jnp.where(hit, near, 0), axis=1, keepdims=True), found)
    own = found < blocks
    count = jnp.sum((kind == 0).astype(jnp.int32), axis=1, keepdims=True)
    table[:TABLE, :] = order
    table[TABLE : 2 * TABLE, :] = jnp.where(own, found, blocks)
    table[2 * TABLE : 3 * TABLE, :] = jnp.where(own, 2 * blocks, found - blocks)
    table[3 * TABLE :, :] = jnp.broadcast_to(count, mine.shape)
    copy(table, out, sem).wait()


def ordered(neighbours):
    return pl.pallas_call(
        order_kernel,
        in_specs=[VMEM],
        out_specs=SMEM,
        out_shape=pltpu.SMEM((4 * TABLE, 128), jnp.int32),
        scratch_shapes=[pltpu.VMEM((4 * TABLE, 128), jnp.int32), DMA],
        compiler_params=params(),
        cost_estimate=LIGHT,
        name="ordered",
    )(neighbours)


def square_part(src, held, low):
    neigh, wide = src.shape[0], held.shape[2]
    piece = [src[:, pl.ds(pl.multiple_of(j * wide, wide), wide)] for j in range(16)]
    held[:, pl.ds(low, 16), :] = jnp.transpose(jnp.stack(piece, axis=0), (1, 0, 2))


def square_kernel(parts, tiles, held, raw, sems):
    count, _, half, wide = held.shape
    each = parts // count
    size = half // each
    loads = []
    for n in range(parts):
        src = tiles.at[n // each, :, pl.ds((n % each) * size * wide, size * wide)]
        loads.append(copy(src, raw.at[n], sems.at[n]))
    for n in range(parts):
        loads[n].wait()

        @pl.loop(0, size // 16)
        def _(step):
            low = pl.multiple_of((n % each) * size + step * 16, 16)
            src = raw.at[n, :, pl.ds(pl.multiple_of(step * 16 * wide, 128), 16 * wide)]
            square_part(src, held.at[n // each], low)


def held_kernel(tiles, held):
    count, _, half, wide = held.shape

    @pl.loop(0, count * (half // 16))
    def _(step):
        b, part = step // (half // 16), step % (half // 16)
        src = tiles.at[b, :, pl.ds(pl.multiple_of(part * 16 * wide, 128), 16 * wide)]
        square_part(src, held.at[b], pl.multiple_of(part * 16, 16))


def squares(tiles, rows):
    count, neigh = tiles.shape[:2]
    half, wide = rows // 2, 2 * rows
    parts = 3 * count
    raw = [pltpu.VMEM((parts, neigh, rows * rows // 3), tiles.dtype), DMA((parts,))]
    return pl.pallas_call(
        functools.partial(square_kernel, parts),
        in_specs=[HBM],
        out_specs=VMEM,
        out_shape=pltpu.VMEM((count, neigh, half, wide), tiles.dtype),
        scratch_shapes=raw,
        compiler_params=params(),
        cost_estimate=HEAVY,
        name="squares",
    )(*in_hbm([tiles]))


def start_near(sides, near, sems):
    copies = []
    cols = near.shape[2] // len(sides)
    for side, chunks in enumerate(sides):
        at = 0
        for chunk in chunks:
            spot = near.at[pl.ds(at, chunk.shape[0]), :, pl.ds(side * cols, cols)]
            copies.append(copy(chunk, spot, sems.at[len(copies)]))
            at += chunk.shape[0]
    near[near.shape[0] - 1] = jnp.zeros(near.shape[1:], near.dtype)
    return copies


def multiply(tiles, table, b, part, first, count, near):
    half, wide = tiles.shape[1:]
    rows = wide // 2
    lane = lax.broadcasted_iota(jnp.int32, (half, 128), 1)
    even = odd = None
    for k in range(first, first + count):
        vec = near[table[part * TABLE + b, k]]
        tile = tiles[table[b, k]]
        mid = tile[:, 128:256]
        none = jnp.zeros_like(mid)
        left = jnp.concatenate([tile[:, :128], jnp.where(lane < PAD, mid, none)], axis=1)
        right = jnp.concatenate([jnp.where(lane < PAD, none, mid), tile[:, 256:]], axis=1)
        one = jnp.concatenate([vec, vec[:PAD]], axis=0)
        two = jnp.concatenate([vec[rows - PAD :], vec], axis=0)
        one = jnp.dot(left, one, preferred_element_type=jnp.float32)
        two = jnp.dot(right, two, preferred_element_type=jnp.float32)
        even = one if even is None else even + one
        odd = two if odd is None else odd + two
    return even, odd


def each_block(held, body):
    first = 0
    for square in held:
        start = first

        @pl.loop(0, square.shape[0])
        def _(n):
            body(start + n, square.at[n])

        first += square.shape[0]


def any_block(needed):
    found = needed(0)
    for b in range(1, BLOCKS):
        found |= needed(b)
    return found


def place(b):
    per = BLOCKS // 2
    core = lax.axis_index("grp") % 2
    return jnp.where(b < per, core * per + b, (1 - core) * per + b - per)


def near_scratch(chunks, sides):
    rows, cols = chunks[0].shape[1:]
    return pltpu.VMEM((sum(c.shape[0] for c in chunks) + 1, rows, sides * cols), chunks[0].dtype)


def slab_kernel(n_other, table, first, tiles, own, *refs):
    other = refs[:n_other]
    acc, second, near, near_sems = refs[-4:]
    held = (first, second)
    loads = start_near(([own], other), near, near_sems)
    held_kernel(tiles, second)
    for load in loads:
        load.wait()

    def body(b, tiles):
        acc[b, 0], acc[b, 1] = multiply(tiles, table, b, 1, 0, 9, near)

    each_block(held, body)
    for group in range(1, 3):
        more = lambda b: table[3 * TABLE + b, 0] > 9 * group

        @pl.when(any_block(more))
        def _():
            def spread(b, tiles):
                @pl.when(more(b))
                def _():
                    even, odd = multiply(tiles, table, b, 1, 9 * group, 9, near)
                    acc[b, 0] += even
                    acc[b, 1] += odd

            each_block(held, spread)


def own_slab(table, held, tiles, own, other):
    cols = own.shape[2]
    return pl.pallas_call(
        functools.partial(slab_kernel, len(other)),
        in_specs=[SMEM] + [VMEM] * 2 + [ANY] * (1 + len(other)),
        out_specs=[VMEM, VMEM],
        out_shape=[
            pltpu.VMEM((BLOCKS, 2, held.shape[2], 2 * cols), jnp.float32),
            pltpu.VMEM(held.shape, held.dtype),
        ],
        scratch_shapes=[near_scratch([own], 2), DMA((1 + len(other),))],
        compiler_params=params(),
        cost_estimate=LIGHT,
        name="own_slab",
    )(in_smem(table), *in_vmem([held, tiles]), own, *other)


def largest(power, size):
    return size * jnp.exp2(power - 14.0)


def few(table):
    return lambda b: table[3 * TABLE + b, 0] < 9


def other_kernel(n_chunks, table, acc, first, second, *refs):
    chunks = refs[:n_chunks]
    out, near, total, image, scales, near_sems = refs[-6:]
    half, rows, cols = first.shape[2], image.shape[0], image.shape[1]
    scales[...] = jnp.zeros_like(scales)
    loads = start_near((chunks,), near, near_sems)
    for n in range(2):
        for b in range(BLOCKS):
            total[b, n] = acc[b, n, :, cols:]
    for load in loads:
        load.wait()

    @pl.when(any_block(few(table)))
    def _():
        def spread(b, tiles):
            @pl.when(few(table)(b))
            def _():
                even, odd = multiply(tiles, table, b, 2, 0, 9, near)
                total[b, 0] += even
                total[b, 1] += odd

        each_block((first, second), spread)

    def body(b, tiles):
        even, odd = multiply(tiles, table, b, 2, 9, 18, near)
        image[pl.ds(0, half, 2), :] = total[b, 0] + even
        image[pl.ds(1, half, 2), :] = total[b, 1] + odd
        value = image[...]
        top = jnp.maximum(jnp.max(jnp.abs(value), axis=0, keepdims=True), 1e-30)
        power = jnp.ceil(jnp.log2(top))
        size = jnp.ceil(top * jnp.exp2(14.0 - power))
        scales[pl.ds(place(b), 1), :] = power
        scales[pl.ds(8 + place(b), 1), :] = size
        value = jnp.round(value * (LEVELS / largest(power, size)))
        rows_out = pl.ds(pl.multiple_of(place(b) * rows, rows), rows)
        out[rows_out, :] = value.astype(jnp.int32).astype(jnp.int16)

    each_block((first, second), body)
    out[pl.ds(BLOCKS * rows, 16), :] = scales[...].astype(jnp.int32).astype(jnp.int16)


def other_images(table, acc, held, chunks, after):
    rows, cols = chunks[0].shape[1:]
    return pl.pallas_call(
        functools.partial(other_kernel, len(chunks)),
        in_specs=[SMEM] + [VMEM] * 3 + [ANY] * (len(chunks) + len(after)),
        out_specs=VMEM,
        out_shape=pltpu.VMEM((BLOCKS * rows + 16, cols), jnp.int16),
        scratch_shapes=[
            near_scratch(chunks, 1),
            pltpu.VMEM((BLOCKS, 2, rows // 2, cols), jnp.float32),
            pltpu.VMEM((rows, cols), jnp.float32),
            pltpu.VMEM((16, cols), jnp.float32),
            DMA((len(chunks),)),
        ],
        compiler_params=params(),
        cost_estimate=LONG,
        name="other_images",
    )(in_smem(table), *in_vmem([acc, *held]), *chunks, *after)


def add_sums(factor, value, probes, cur, sums):
    for n, term in enumerate((probes * value, cur.astype(jnp.float32) * value)):
        part = jnp.sum(term.reshape(-1, 8, term.shape[-1]), axis=0) * factor
        sums[pl.ds(8 * n, 8), :] += part


def own_kernel(n_chunks, factor, table, acc, first_held, second_held, *refs):
    chunks, rows_in = refs[:n_chunks], refs[n_chunks : n_chunks + 3]
    out, sums, *later = refs[n_chunks + 4 : n_chunks + 9]
    near, image, prev, probes, cur, near_sems, row_sems, later_sems, out_sems = refs[-9:]
    half = first_held.shape[2]
    loads = start_near((chunks,), near, near_sems)
    cols = image.shape[2]
    first = (lax.axis_index("grp") // 2) * BLOCKS
    mine = []
    for n, (src, dst) in enumerate(zip(rows_in, (prev, probes, cur))):
        mine.append(copy(src.at[pl.ds(first, BLOCKS)], dst, row_sems.at[n]))
    sums[...] = jnp.zeros_like(sums)
    for made in loads:
        made.wait()

    def body(b, tiles):
        at = place(b)
        even, odd = multiply(tiles, table, b, 2, 9, 18, near)
        image[b, pl.ds(0, half, 2), :] = acc[b, 0, :, :cols] + even
        image[b, pl.ds(1, half, 2), :] = acc[b, 1, :, :cols] + odd

        @pl.when(few(table)(b))
        def _():
            even, odd = multiply(tiles, table, b, 2, 0, 9, near)
            image[b, pl.ds(0, half, 2), :] += even
            image[b, pl.ds(1, half, 2), :] += odd

        @pl.when(b == 0)
        def _():
            for made in mine:
                made.wait()
            for n, (src, dst) in enumerate(zip(rows_in, later)):
                copy(src.at[pl.ds(BLOCKS - first, BLOCKS)], dst, later_sems.at[n])

        value = 2.0 * image[b] - prev[at]
        image[b] = value
        copy(image.at[b], out.at[first + at], out_sems.at[b])
        add_sums(factor, value, probes[at], cur[at], sums)

    each_block((first_held, second_held), body)
    for n, (src, dst) in enumerate(zip(rows_in, later)):
        pltpu.make_async_copy(src.at[pl.ds(BLOCKS - first, BLOCKS)], dst, later_sems.at[n]).wait()
    for b in range(BLOCKS):
        pltpu.make_async_copy(image.at[b], out.at[first + place(b)], out_sems.at[b]).wait()


def own_rows(table, acc, held, chunks, factor, prev, probes, cur, after):
    rows, cols = cur.shape[1:]
    part = (BLOCKS, rows, cols)
    return pl.pallas_call(
        functools.partial(own_kernel, len(chunks), factor),
        in_specs=[SMEM] + [VMEM] * 3 + [ANY] * (len(chunks) + 3 + len(after)),
        out_specs=[HBM] + [VMEM] * 4,
        out_shape=[
            pltpu.HBM(prev.shape, jnp.float32),
            pltpu.VMEM((16, cols), jnp.float32),
            pltpu.VMEM(part, jnp.float32),
            pltpu.VMEM(part, jnp.float32),
            pltpu.VMEM(part, cur.dtype),
        ],
        scratch_shapes=[
            near_scratch(chunks, 1),
            pltpu.VMEM(part, jnp.float32),
            pltpu.VMEM(part, jnp.float32),
            pltpu.VMEM(part, jnp.float32),
            pltpu.VMEM(part, cur.dtype),
            DMA((len(chunks),)),
            DMA((3,)),
            DMA((3,)),
            DMA((BLOCKS,)),
        ],
        compiler_params=params(),
        cost_estimate=LONG,
        name="own_rows",
    )(in_smem(table), *in_vmem([acc, *held]), *chunks, prev, probes, cur, *after)


def final_kernel(factor, coded, prev, probes, cur, sums_in, _, out, sums, value, acc, sem):
    rows = prev.shape[1]
    scales = coded[pl.ds(BLOCKS * rows, 16), :].astype(jnp.int32).astype(jnp.float32)
    step = largest(scales[:8], scales[8:]) * (1.0 / LEVELS)
    for b in range(BLOCKS):
        image = coded[pl.ds(b * rows, rows), :].astype(jnp.int32).astype(jnp.float32) * step[b : b + 1]
        value[b] = 2.0 * image - prev[b]
    first = (1 - lax.axis_index("grp") // 2) * BLOCKS
    send = copy(value, out.at[pl.ds(first, BLOCKS)], sem)
    acc[...] = sums_in[...]
    for b in range(BLOCKS):
        add_sums(factor, value[b], probes[b], cur[b], acc)
    for n in range(2):
        sums[pl.ds(n, 1), :] = jnp.sum(acc[pl.ds(8 * n, 8), :], axis=0, keepdims=True)
    send.wait()


def other_rows(factor, coded, prev, probes, cur, t_next, sums):
    cols = cur.shape[2]
    return pl.pallas_call(
        functools.partial(final_kernel, factor),
        in_specs=[VMEM] * 5 + [HBM],
        out_specs=[HBM, VMEM],
        out_shape=[
            pltpu.HBM(t_next.shape, jnp.float32),
            jax.ShapeDtypeStruct((2, cols), jnp.float32),
        ],
        scratch_shapes=[pltpu.VMEM(prev.shape, jnp.float32), pltpu.VMEM((16, cols), jnp.float32), DMA],
        input_output_aliases={5: 0},
        compiler_params=params(),
        cost_estimate=LIGHT,
        name="other_rows",
    )(*in_vmem([coded, prev, probes, cur, sums]), *in_hbm([t_next]))


def gate(value, *after):
    return pl.pallas_call(
        lambda *refs: None,
        in_specs=[ANY] + [SMEM if a.dtype == jnp.int32 else ANY for a in after],
        out_specs=ANY,
        out_shape=jax.ShapeDtypeStruct(value.shape, value.dtype),
        input_output_aliases={0: 0},
        compiler_params=params(),
        cost_estimate=LIGHT,
        name="gate",
    )(value, *[in_smem(a) if a.dtype == jnp.int32 else a for a in after])


def sum_over(value, axis):
    size = lax.axis_size(axis)
    if size & (size - 1):
        return lax.psum(value, axis)
    value, hop = value + lax.ppermute(value, axis, [(i, i ^ 1) for i in range(size)]), 2
    while hop < size:
        jumps = (3 * hop, hop, 2 * hop) if 2 * hop < size else (hop,)
        far = [lax.ppermute(value, axis, [(i, i ^ j) for i in range(size)]) for j in jumps]
        value = value + far[0]
        if len(far) > 1:
            value = value + (far[1] + far[2])
        hop *= len(jumps) + 1
    return value


def shards(tiles, neighbours, t_cur, t_prev, probes):
    blocks, rows, cols = t_cur.shape
    per = tiles.shape[0]
    slabs, lanes = lax.axis_size("slab"), lax.axis_size("grp")
    factor = 1.0 / math.sqrt(slabs * blocks * rows)
    across = functools.partial(lax.ppermute, axis_name="grp", perm=[(i, i ^ 2) for i in range(lanes)])
    sibling = functools.partial(lax.ppermute, axis_name="grp", perm=[(i, i ^ 1) for i in range(lanes)])
    pair = functools.partial(lax.ppermute, axis_name="slab", perm=[(i, i ^ 1) for i in range(slabs)])
    along = functools.partial(
        lax.ppermute,
        axis_name="slab",
        perm=[(i, (i + 2 if i % 2 == 0 else i - 2) % slabs) for i in range(slabs)],
    )

    tiles, t_prev, probes, fixed = in_hbm([tiles, t_prev, probes, t_cur])
    half = blocks // 2
    low, high = t_cur[:half], t_cur[half:]

    sib_tiles = sibling(tiles)
    oth = [across(low), across(high)]
    near_high = pair(high)
    table = ordered(neighbours)
    held = squares(tiles, rows)
    oth[0] = gate(oth[0], held, table)
    near_oth = [pair(oth[0]), pair(oth[1])]
    far_high = along(near_high)
    far_oth = [along(near_oth[0]), across(far_high)]
    acc, sib_held = own_slab(table, held, sib_tiles, fixed, oth)
    held = [held, sib_held]
    far_oth[0] = gate(far_oth[0], acc)
    near_low = pair(gate(low, acc))
    far_low = across(far_oth[0])

    images = other_images(table, acc, held, [*near_oth, *far_oth], ())
    images = gate(images, near_low, far_low)
    back = across(images)
    own = [near_low, near_high, far_low, far_high]
    t_next, sums, *later = own_rows(table, acc, held, own, factor, t_prev, probes, fixed, [images])
    t_next, sums = other_rows(factor, back, *later, t_next, sums)
    return (t_next, sum_over(sums, "slab"))


def solution(mesh):
    placed = (
        P(("slab", "grp"), None, None),
        P("slab", None),
        P("slab", None, "grp"),
        P("slab", None, "grp"),
        P("slab", None, "grp"),
    )
    return jax.shard_map(
        shards,
        mesh=mesh,
        in_specs=placed,
        out_specs=(P("slab", None, "grp"), P(None, "grp")),
        check_vma=False,
    )
```
